128 devices in a mesh: batch: 8 (over z_lo, y), blk: 16 (over x, z_hi, core).
Axes of the slice: x: 4, y: 4, z: 4 (z_hi: 2, z_lo: 2; z = z_hi * 2 + z_lo), core: 2. Of those that a mesh axis runs over, the one named last changes fastest.
Arguments:
- tokens: bfloat16 [16, 1024, 512], P('batch', 'blk'), may hold values from -6 to 6
- patches: bfloat16 [16, 1280, 384], P('batch', 'blk'), may hold values from -6 to 6
- camera: bfloat16 [16, 1024], P('batch'), may hold values from -6 to 6
- counts: int32 [16], P('batch'), may hold values from 160 to 1280, as said below
- grad_out: bfloat16 [16, 1024, 512], P('batch', 'blk'), may hold values from -6 to 6
- w_mod: bfloat16 [1024, 1024], P('blk'), may hold values from -0.09375 to 0.09375
- w_query: bfloat16 [512, 512], P('blk'), may hold values from -0.25 to 0.25
- w_key: bfloat16 [512, 512], P('blk'), may hold values from -0.25 to 0.25
- w_value: bfloat16 [512, 512], P('blk'), may hold values from -0.25 to 0.25
- w_out: bfloat16 [512, 512], P('blk'), may hold values from -3 to 3
- w_patch: bfloat16 [384, 512], P('blk'), may hold values from -0.3125 to 0.3125
- c_query: bfloat16 [512, 512], P('blk'), may hold values from -0.25 to 0.25
- c_key: bfloat16 [512, 512], P('blk'), may hold values from -0.25 to 0.25
- c_value: bfloat16 [512, 512], P('blk'), may hold values from -0.25 to 0.25
- c_out: bfloat16 [512, 512], P('blk'), may hold values from -3 to 3
- gain_two: bfloat16 [512], P('blk'), may hold values from 0.5 to 1.5
- bias_two: bfloat16 [512], P('blk'), may hold values from -2 to 2
- gain_three: bfloat16 [512], P('blk'), may hold values from 0.5 to 1.5
- bias_three: bfloat16 [512], P('blk'), may hold values from -2 to 2
- w_up: bfloat16 [512, 2048], P('blk'), may hold values from -0.25 to 0.25
- w_down: bfloat16 [2048, 512], P('blk'), may hold values from -0.125 to 0.125
Outputs:
- out_tokens: bfloat16 [16, 1024, 512], P('batch', 'blk')
- grad_tokens: bfloat16 [16, 1024, 512], P('batch', 'blk')
- grad_patches: bfloat16 [16, 1280, 384], P('batch', 'blk')
- grad_mod: float32 [1024, 1024], P(('batch', 'blk'))
- grad_query: float32 [512, 512], P(('batch', 'blk'))
- grad_key: float32 [512, 512], P(('batch', 'blk'))
- grad_value: float32 [512, 512], P(('batch', 'blk'))
- grad_out_proj: float32 [512, 512], P(('batch', 'blk'))
- grad_patch_proj: float32 [384, 512], P(('batch', 'blk'))
- grad_cquery: float32 [512, 512], P(('batch', 'blk'))
- grad_ckey: float32 [512, 512], P(('batch', 'blk'))
- grad_cvalue: float32 [512, 512], P(('batch', 'blk'))
- grad_cout: float32 [512, 512], P(('batch', 'blk'))
- grad_gain_two: float32 [512], P(('batch', 'blk'))
- grad_bias_two: float32 [512], P(('batch', 'blk'))
- grad_gain_three: float32 [512], P(('batch', 'blk'))
- grad_bias_three: float32 [512], P(('batch', 'blk'))
- grad_up: float32 [512, 2048], P(('batch', 'blk'))
- grad_down: float32 [2048, 512], P(('batch', 'blk'))
The draws below stay inside these ranges and needn't reach their ends.
Inputs may be any that keep to these rules, and one draw needn't show every extreme that they name: counts[o] is 1280 // k for some k from 1 to 8; in every group of 2 consecutive objects one object has all 1280 slots live.
All inputs are finite; a program needn't handle non-finite values.
Results may differ from the reference program's by a relative error of at most 0.028.
Values may be sent and summed in bfloat16 or wider, within the bound.
A program may use at most 128 MiB of HBM per device.

```python
import jax
import jax.numpy as jnp
from jax import lax

D = 512
HEADS = 8
HEAD_DIM = 64
FF = 2048
PD = 384
CAM = 1024
MB = 2
OBJECTS = 16
SEQ = 1024
PMAX = 1280


def draw_counts(key, part):
    key = jax.random.fold_in(key, 7)
    key_div, key_full = jax.random.split(key)
    divisor = jax.random.randint(key_div, (OBJECTS,), 1, 9)
    partial_counts = PMAX // divisor
    chosen = jax.random.randint(key_full, (OBJECTS // MB,), 0, MB)
    chosen_rows = jnp.repeat(chosen, MB)
    slot_index = jnp.arange(OBJECTS, dtype=jnp.int32) % MB
    return jnp.where(slot_index == chosen_rows, PMAX, partial_counts).astype(jnp.int32)


def shard_levels(rng, dims, pieces, low, top_value):
    gain = 1.0
    for axis_at, shards_of in pieces:
        draws = jax.random.uniform(jax.random.fold_in(jax.random.fold_in(rng, 6), axis_at), (shards_of,), jnp.float32, low / len(pieces), top_value / len(pieces))
        gain = gain * jnp.repeat(jnp.exp(draws), dims[axis_at] // shards_of).reshape((-1,) + (1,) * (len(dims) - 1 - axis_at))
    return gain


def bell_draw(key, extent, scale, reach, pieces=(), kind=jnp.bfloat16):
    values = scale * jax.random.normal(key, extent, jnp.float32)
    if pieces:
        values = values * shard_levels(key, extent, pieces, -0.22, 0.18)
    return jnp.clip(values, -reach, reach).astype(kind)


def setup_inputs(seed: int = 0) -> dict:
    key_of = jax.random.split(jax.random.key(seed), 22)
    return {
        "tokens": bell_draw(key_of[0], (OBJECTS, SEQ, D), 1.0, 6.0, ((0, 8), (1, 16))),
        "patches": bell_draw(key_of[1], (OBJECTS, PMAX, PD), 1.0, 6.0, ((0, 8), (1, 16))),
        "camera": bell_draw(key_of[2], (OBJECTS, CAM), 1.0, 6.0, ((0, 8),)),
        "counts": draw_counts(jax.random.fold_in(key_of[21], 71), 0),
        "grad_out": bell_draw(key_of[4], (OBJECTS, SEQ, D), 1.0, 6.0, ((0, 8), (1, 16))),
        "w_mod": bell_draw(key_of[5], (CAM, 2 * D), (4 * CAM) ** -0.5, 0.09375, ((0, 16),)),
        "w_query": bell_draw(key_of[6], (D, D), D ** -0.5, 0.25, ((0, 16),)),
        "w_key": bell_draw(key_of[7], (D, D), D ** -0.5, 0.25, ((0, 16),)),
        "w_value": bell_draw(key_of[8], (D, D), D ** -0.5, 0.25, ((0, 16),)),
        "w_out": bell_draw(key_of[9], (D, D), 0.5, 3.0, ((0, 16),)),
        "w_patch": bell_draw(key_of[10], (PD, D), PD ** -0.5, 0.3125, ((0, 16),)),
        "c_query": bell_draw(key_of[11], (D, D), D ** -0.5, 0.25, ((0, 16),)),
        "c_key": bell_draw(key_of[12], (D, D), D ** -0.5, 0.25, ((0, 16),)),
        "c_value": bell_draw(key_of[13], (D, D), D ** -0.5, 0.25, ((0, 16),)),
        "c_out": bell_draw(key_of[14], (D, D), 0.5, 3.0, ((0, 16),)),
        "gain_two": jnp.clip(1.0 + 0.1 * jax.random.normal(key_of[15], (D,), jnp.float32), 0.5, 1.5).astype(jnp.bfloat16),
        "bias_two": bell_draw(key_of[16], (D,), 0.3, 2.0, ((0, 16),)),
        "gain_three": jnp.clip(1.0 + 0.1 * jax.random.normal(key_of[17], (D,), jnp.float32), 0.5, 1.5).astype(jnp.bfloat16),
        "bias_three": bell_draw(key_of[18], (D,), 0.3, 2.0, ((0, 16),)),
        "w_up": bell_draw(key_of[19], (D, FF), D ** -0.5, 0.25, ((0, 16),)),
        "w_down": bell_draw(key_of[20], (FF, D), FF ** -0.5, 0.125, ((0, 16),)),
    }


@jax.custom_vjp
def low(v):
    return lax.optimization_barrier(v.astype(jnp.bfloat16)).astype(jnp.float32)

@jax.custom_vjp
def low_back(v):
    return v

def low_keep(v):
    return (low(v), None)

def low_pass(kept, grad):
    return (grad,)

def back_keep(v):
    return (v, None)

def back_low(kept, grad):
    return (low(grad),)
low.defvjp(low_keep, low_pass)
low_back.defvjp(back_keep, back_low)
EPSILON = 1e-05
HIGH = lax.Precision.HIGHEST

def product(left, right):
    return jnp.dot(left, right, precision=HIGH)

def both_round(value):
    return low_back(low(value))

def layer_norm(stream):
    centred = stream - lax.optimization_barrier(jnp.mean(stream, -1, keepdims=True))
    return centred * lax.rsqrt(lax.optimization_barrier(jnp.mean(centred * centred, -1, keepdims=True)) + EPSILON)

def attention(queries, keys, values, in_range):
    query_heads = queries.reshape(queries.shape[0], HEADS, HEAD_DIM)
    key_heads = keys.reshape(keys.shape[0], HEADS, HEAD_DIM)
    value_heads = values.reshape(values.shape[0], HEADS, HEAD_DIM)
    scores = low_back(jnp.einsum('thd,shd->hts', query_heads, key_heads, precision=HIGH) * HEAD_DIM ** (-0.5))
    scores = jnp.where(in_range[None, None, :], scores, -1e+30)
    weights = jax.nn.softmax(scores, axis=-1)
    mixed = jnp.einsum('hts,shd->thd', low(weights), value_heads, precision=HIGH)
    return mixed.reshape(queries.shape[0], HEADS * HEAD_DIM)

def one_object(params, stream, patch_rows, camera_row, count_now):
    w_mod, w_query, w_key, w_value, w_out, w_patch, c_query, c_key, c_value, c_out, gain_two, bias_two, gain_three, bias_three, w_up, w_down = params
    modulation = product(camera_row, w_mod)
    scale_part = modulation[:D]
    shift_part = modulation[D:]
    first_in = low(layer_norm(stream) * (1.0 + scale_part) + shift_part)
    queries = both_round(product(first_in, w_query))
    keys = both_round(product(first_in, w_key))
    values = both_round(product(first_in, w_value))
    every_key = lax.iota(jnp.int32, stream.shape[0]) >= 0
    self_mixed = both_round(attention(queries, keys, values, every_key))
    after_self = stream + low_back(product(self_mixed, w_out))
    second_in = low(layer_norm(after_self) * gain_two + bias_two)
    cross_queries = both_round(product(second_in, c_query))
    projected = both_round(product(patch_rows, w_patch))
    cross_keys = both_round(product(projected, c_key))
    cross_values = both_round(product(projected, c_value))
    live_slots = lax.iota(jnp.int32, patch_rows.shape[0]) < count_now
    cross_mixed = both_round(attention(cross_queries, cross_keys, cross_values, live_slots))
    after_cross = after_self + low_back(product(cross_mixed, c_out))
    third_in = low(layer_norm(after_cross) * gain_three + bias_three)
    hidden_pre = both_round(product(third_in, w_up))
    hidden_act = both_round(jax.nn.gelu(hidden_pre))
    return after_cross + low_back(product(hidden_act, w_down))

def reference(tokens, patches, camera, counts, grad_out, w_mod, w_query, w_key, w_value, w_out, w_patch, c_query, c_key, c_value, c_out, gain_two, bias_two, gain_three, bias_three, w_up, w_down):
    camera_wide = camera.astype(jnp.float32)

    def forward(stream_all, patch_all, p_mod, p_query, p_key, p_value, p_out, p_patch, q_cross, k_cross, v_cross, o_cross, g_two, b_two, g_three, b_three, p_up, p_down):
        params = (p_mod, p_query, p_key, p_value, p_out, p_patch, q_cross, k_cross, v_cross, o_cross, g_two, b_two, g_three, b_three, p_up, p_down)

        def run_object(items):
            return one_object(params, items[0], items[1], items[2], items[3])
        return lax.map(jax.checkpoint(run_object), (stream_all, patch_all, camera_wide, counts))
    inputs = (tokens, patches, w_mod, w_query, w_key, w_value, w_out, w_patch, c_query, c_key, c_value, c_out, gain_two, bias_two, gain_three, bias_three, w_up, w_down)
    wide = tuple((item.astype(jnp.float32) for item in inputs))
    result, pullback = jax.vjp(forward, *wide)
    g_tokens, g_patches, g_mod, g_query, g_key, g_value, g_out, g_patch, g_cquery, g_ckey, g_cvalue, g_cout, g_gain_two, g_bias_two, g_gain_three, g_bias_three, g_up, g_down = pullback(grad_out.astype(jnp.float32))
    return (result.astype(jnp.bfloat16), g_tokens.astype(jnp.bfloat16), g_patches.astype(jnp.bfloat16), g_mod, g_query, g_key, g_value, g_out, g_patch, g_cquery, g_ckey, g_cvalue, g_cout, g_gain_two, g_bias_two, g_gain_three, g_bias_three, g_up, g_down)
```

```python
import enum
import functools
import types

import jax
import jax.numpy as jnp
from jax import lax
from jax.experimental import pallas as pl
from jax.experimental.pallas import tpu as pltpu
from jax.sharding import PartitionSpec as P

F32 = jnp.float32
BF = jnp.bfloat16
MESH = pl.DeviceIdType.MESH
EPSILON = 1e-05
BIG_NEG = -1e30
GELU_K = 0.7978845608028654
GELU_C = 0.044715


def dot(left, right):
    return jnp.dot(left, right, preferred_element_type=F32)


def dot_nt(left, right):
    return lax.dot_general(left, right, (((1,), (1,)), ((), ())), preferred_element_type=F32)


def dot_tn(left, right):
    return lax.dot_general(left, right, (((0,), (0,)), ((), ())), preferred_element_type=F32)


def normalize(stream):
    centred = stream - jnp.mean(stream, -1, keepdims=True)
    inverse = lax.rsqrt(jnp.mean(centred * centred, -1, keepdims=True) + EPSILON)
    return centred * inverse, inverse


def norm_back(dnormed, normed, inverse):
    return inverse * (
        dnormed
        - jnp.mean(dnormed, -1, keepdims=True)
        - normed * jnp.mean(dnormed * normed, -1, keepdims=True)
    )


def column_sum(rows):
    return jnp.sum(rows, 0, keepdims=True)


def iota(shape, dim):
    return lax.broadcasted_iota(jnp.int32, shape, dim)


class Inputs:
    tok = pltpu.VMEM
    pat = pltpu.VMEM
    camera = pltpu.VMEM
    counts = pltpu.SMEM
    go = pltpu.VMEM
    w_mod = pltpu.VMEM
    w_query = pltpu.VMEM
    w_key = pltpu.VMEM
    w_value = pltpu.VMEM
    w_out = pltpu.VMEM
    w_patch = pltpu.VMEM
    c_query = pltpu.VMEM
    c_key = pltpu.VMEM
    c_value = pltpu.VMEM
    c_out = pltpu.VMEM
    gb = pltpu.VMEM
    w_up = pltpu.VMEM
    w_down = pltpu.VMEM


class Outputs:
    out_tok = ((2, 64, 512), BF)
    g_tok = ((2, 64, 512), BF)
    g_pat = ((2, 80, 384), BF)
    g_mod = ((8, 1024), F32)
    g_query = ((4, 512), F32)
    g_key = ((4, 512), F32)
    g_value = ((4, 512), F32)
    g_out = ((4, 512), F32)
    g_patch = ((3, 512), F32)
    g_cquery = ((4, 512), F32)
    g_ckey = ((4, 512), F32)
    g_cvalue = ((4, 512), F32)
    g_cout = ((4, 512), F32)
    g_up = ((4, 2048), F32)
    g_down = ((16, 512), F32)
    g_vec = ((4, 512), F32)


class Scratch:
    cam = ((16, 128), F32)
    tokh = ((8, 64, 512), BF)
    path = ((8, 80, 384), BF)
    wqs = ((4, 32, 384), BF)
    wfs = ((32, 1664), BF)
    wqkv = ((8, 2, 32, 384), BF)
    wf = ((8, 2, 32, 1664), BF)
    mods = ((2, 8, 128), F32)
    modr = ((8, 8, 128), F32)
    modo = ((8, 128), F32)
    modx = ((8, 128), F32)
    camr = ((8, 16, 128), F32)
    gv = ((8, 512), F32)
    bias = ((1280, 128), F32)
    n1h = ((4, 128, 512), F32)
    a1h = ((4, 128, 512), BF)
    qs = ((4, 128, 128), BF)
    kv = ((2, 4, 128, 256), BF)
    p1 = ((4, 1024, 256), BF)
    o1s = ((4, 128, 128), BF)
    o1r = ((4, 128, 128), BF)
    x1 = ((128, 512), F32)
    n2 = ((128, 512), F32)
    i2 = ((128, 128), F32)
    a2 = ((128, 512), BF)
    wk = ((8, 2, 32, 1536), BF)
    kvc = ((2, 4, 160, 1024), BF)
    p2 = ((4, 1280, 256), BF)
    x2 = ((128, 512), F32)
    n3 = ((128, 512), F32)
    i3 = ((128, 128), F32)
    das = ((128, 512), BF)
    dar = ((128, 512), BF)
    ops = ((128, 512), BF)
    opr = ((128, 512), BF)
    outs = ((2, 64, 512), BF)
    dx2 = ((128, 512), F32)
    dkvc = ((2, 4, 160, 1024), BF)
    dkcr = ((4, 160, 1024), BF)
    gps = ((4, 160, 384), BF)
    gpr = ((4, 160, 384), BF)
    gpo = ((2, 80, 384), BF)
    dx1 = ((128, 512), F32)
    do1s = ((4, 128, 128), BF)
    do1r = ((4, 128, 128), BF)
    dkv = ((2, 512, 256), F32)
    dkvs = ((512, 256), BF)
    dkvr = ((512, 256), BF)
    dqkv = ((512, 384), BF)
    d1s = ((4, 128, 512), BF)
    d1r = ((4, 128, 512), BF)
    gts = ((2, 64, 512), BF)
    dq = ((4, 128, 128), BF)
    gb2 = ((512, 512), F32)
    gbs = ((512, 512), BF)
    gbr = ((512, 512), BF)
    gc = ((512, 384), F32)
    e1s = ((16, 32, 1024), BF)
    e1r = ((16, 32, 1024), BF)
    e2s = ((16, 32, 1280), BF)
    e2r = ((16, 32, 1280), BF)
    e3s = ((16, 32, 384), BF)
    e3r = ((16, 32, 384), BF)
    u1o = ((8, 1024), F32)
    u1z = ((8, 1024), F32)
    dns = ((2, 32, 512), F32)
    dnr = ((4, 32, 512), F32)
    dnz = ((16, 512), F32)
    u2s = ((32, 1536), F32)
    u2r = ((4, 8, 1536), F32)
    u2o = ((8, 1536), F32)
    u2z = ((8, 1536), F32)
    u3s = ((32, 384), F32)
    u3r = ((4, 8, 384), F32)
    u3z = ((4, 8, 384), F32)
    tb = ((24, 128), F32)
    tbs = ((24, 128), F32)
    tbx = ((24, 128), F32)
    tbr = ((4, 24, 128), F32)
    tbo = ((24, 128), F32)
    tbp = ((16, 24, 128), F32)
    wks = ((32, 1536), BF)
    kt = ((128, 1024), BF)
    vt = ((128, 1024), BF)
    wp = ((384, 512), BF)
    pp = ((4, 160, 512), BF)
    qc = ((4, 128, 128), BF)
    o2 = ((4, 128, 128), BF)
    do2 = ((4, 128, 128), BF)
    dqc = ((4, 128, 128), BF)
    dks = ((4, 160, 1024), BF)
    dpp = ((4, 160, 512), BF)
    w3s = ((32, 1024), BF)
    w3m = ((2, 32, 1024), BF)
    w3 = ((8, 2, 32, 1024), BF)
    w4 = ((8, 128, 512), BF)
    go2 = ((2, 2, 64, 512), BF)
    a32 = ((2, 128, 512), BF)
    g2 = ((2, 128, 1024), BF)
    du2 = ((2, 128, 1024), BF)
    dao = ((128, 512), F32)
    oo = ((128, 512), F32)
    dno = ((32, 512), F32)
    gus = ((8, 4, 16, 1024), BF)
    gur = ((4, 8, 16, 1024), BF)
    ga = ((512, 1024), F32)
    gas = ((512, 1024), BF)
    gar = ((512, 1024), BF)
    e4s = ((16, 32, 512), BF)
    e4r = ((16, 32, 512), BF)


def members(group):
    return {name: value for name, value in vars(group).items() if not name.startswith("_")}


INPUTS, OUTPUTS, SCRATCH = members(Inputs), members(Outputs), members(Scratch)


class K(enum.IntEnum):
    a3 = 0
    cam = 1
    d1 = 2
    da = 3
    dkc = 4
    dkv = 5
    dn0 = 6
    dn1 = 7
    dnr = 8
    dnz = 9
    do1 = 10
    e1 = 11
    e2 = 12
    e3 = 13
    e4 = 14
    ga = 15
    gb = 16
    go = 17
    gox = 18
    gp = 19
    gpz = 20
    gt = 21
    kv = 22
    kvc = 23
    mod = 24
    modx = 25
    o1 = 26
    op = 27
    out = 28
    pat = 29
    tbp = 30
    tbs = 31
    tbx = 32
    tok = 33
    u1z = 34
    u2 = 35
    u2z = 36
    u3 = 37
    u3z = 38
    ux = 39
    w1a = 40
    w1b = 41
    w1c = 42
    w1d = 43
    w2 = 44
    w2d = 45
    w3 = 46
    w3x = 47
    w4a = 48
    w4b = 49
    w4c = 50
    wq = 51
    wqx = 52


def kernel(*refs):
    *buffers, ss, rs = refs
    R = types.SimpleNamespace(**dict(zip((*INPUTS, *OUTPUTS, *SCRATCH), buffers)))
    b = lax.axis_index("batch")
    j = lax.axis_index("blk")
    x = j // 4
    t = (j // 2) % 2
    c = j % 2
    p = 2 * x + t
    i_me = 2 * b + t

    def did(bb, xx, tt, cc):
        return (bb, xx * 4 + tt * 2 + cc)

    pending = []
    do1_base = len(K)

    def push(name, src, dst, dev, slot=None):
        pltpu.make_async_remote_copy(
            src_ref=src,
            dst_ref=dst,
            send_sem=ss.at[name],
            recv_sem=rs.at[name if slot is None else slot],
            device_id=dev,
            device_id_type=MESH,
        ).start()

    def got(name, like):
        pltpu.make_async_copy(like, like, rs.at[name]).wait()

    def sent(name, like):
        pltpu.make_async_copy(like, like, ss.at[name]).wait()

    def later(name, like, when=None):
        pending.append((name, like, when))

    sibling = did(b, x, t, 1 - c)
    partner = did(b, x, 1 - t, c)
    near = [((x + dx) % 4, (t + dt) % 2) for dx, dt in ((0, 1), (1, 0), (3, 0), (2, 0), (1, 1), (3, 1), (2, 1))]

    def near_push(name, src_of, dst, like):
        for xx, tt in near:
            push(name, src_of(xx, tt), dst, did(b, xx, tt, c))
        later(name, like)

    def x_push(name, src_of, dst_ref):
        for d in (1, 3, 2):
            xx = (x + d) % 4
            push(name, src_of(xx), dst_ref.at[x], did(b, xx, t, c))
        later(name, dst_ref.at[0:3])

    def x_got(name, dst_ref):
        got(name, dst_ref.at[0:3])

    def sib_push(name, src, dst):
        push(name, src, dst, sibling)
        later(name, dst)

    def plane_push(name, src, dst):
        def step(n, carry):
            bb = (b + n // 2) % 8
            tt = (t + n % 2) % 2
            pltpu.make_async_remote_copy(
                src_ref=src.at[2 * bb + tt] if src.shape[0] == 16 else src,
                dst_ref=dst.at[i_me],
                send_sem=ss.at[name],
                recv_sem=rs.at[name],
                device_id=did(bb, x, tt, c),
                device_id_type=MESH,
            ).start()
            return carry

        lax.fori_loop(1, 16, step, 0)
        later(name, dst.at[0:15])

    def plane_sum(ref):
        def step(n, acc):
            return acc + ref[n].astype(F32)

        return lax.fori_loop(1, 16, step, ref[0].astype(F32))

    for i in range(4):
        cols = slice(128 * i, 128 * i + 128)
        R.wqs[i, :, 0:128] = R.w_query[:, cols]
        R.wqs[i, :, 128:256] = R.w_key[:, cols]
        R.wqs[i, :, 256:384] = R.w_value[:, cols]
    lanes = iota((1, 128), 1)
    half = jnp.where(lanes // 64 == c, 1.0, 0.0).astype(F32)
    for o in range(2):
        for i in range(8):
            R.cam[8 * o + i : 8 * o + i + 1, :] = R.camera[o : o + 1, 128 * i : 128 * i + 128].astype(F32)
    row0 = R.cam[pl.ds(j // 2, 1), :] * half
    row1 = R.cam[pl.ds(8 + j // 2, 1), :] * half
    rows = jnp.concatenate([row0, row1, jnp.zeros((14, 128), F32)], 0).astype(BF)
    w_mod = R.w_mod[...]
    modp = dot(rows, jnp.concatenate([w_mod, w_mod], 0))
    for i in range(8):
        R.mods[0, i : i + 1, :] = modp[0:1, 128 * i : 128 * i + 128]
        R.mods[1, i : i + 1, :] = modp[1:2, 128 * i : 128 * i + 128]

    bar = pltpu.get_barrier_semaphore()

    def greet(dev):
        pl.semaphore_signal(bar, inc=1, device_id=dev, device_id_type=MESH)

    for xx, tt in near:
        greet(did(b, xx, tt, c))
    greet(sibling)

    def greet_plane(n, carry):
        greet(did((b + n // 2) % 8, x, (t + n % 2) % 2, c))
        return carry

    lax.fori_loop(1, 16, greet_plane, 0)

    pl.semaphore_wait(bar, 7 + 1 + 15)

    near_push(K.mod, lambda xx, tt: R.mods.at[tt], R.modr.at[p], R.modr.at[0:7])
    near_push(K.tok, lambda xx, tt: R.tok.at[tt], R.tokh.at[p], R.tokh.at[0:7])
    near_push(K.wq, lambda xx, tt: R.wqs.at[xx], R.wqkv.at[p, c], R.wqkv.at[0:7, 0])

    y = b % 4
    xs = (x + y) % 4
    xd = (x + 4 - y) % 4

    def spread_first(same, cross, src, whole):
        push(cross, src, slot(whole, p), did(b, xd, 1 - t, c))
        later(cross, src)

        @pl.when(y > 0)
        def _():
            push(same, src, slot(whole, p), did(b, xd, t, c))

        later(same, src, y > 0)

        @pl.when(y == 0)
        def _():
            slot(whole, p)[...] = src[...]

    def spread_second(same, cross, name, whole):
        got(cross, slot(whole, 0))

        @pl.when(y > 0)
        def _():
            got(same, slot(whole, 0))

        held = slot(whole, pl.ds(2 * xs, 2))
        for d in (2, 1, 3):
            push(name, held, held, did(b - y + (y + d) % 4, x, t, c))
        later(name, slot(whole, slice(0, 6)))

    def slot(whole, at):
        return whole.at[at, c] if len(whole.shape) == 4 else whole.at[at]

    def spread_third(name, whole):
        got(name, slot(whole, slice(0, 6)))

    def spread_last(name, whole):
        sib_push(name, whole.at[:, c], whole.at[:, c])

    f = iota((32, 24), 1)
    apart = jnp.where(iota((32, 24), 0) == f + (f * 21846) // 65536, 1.0, 0.0).astype(BF)
    R.wks[:, 0:512] = R.c_key[...]
    R.wks[:, 512:1024] = R.c_value[...]
    R.wks[:, 1024:1536] = dot(apart, R.w_patch[...]).astype(BF)
    R.wfs[:, 0:512] = R.w_out[...]
    R.wfs[:, 512:1024] = R.c_query[...]
    R.wfs[:, 1024:1536] = R.c_out[...]
    R.wfs[:, 1536:1664] = R.gb[...]
    for i in range(8):
        left, right = R.w_up[:, 256 * i : 256 * i + 128], R.w_up[:, 256 * i + 128 : 256 * i + 256]
        R.w3s[:, 128 * i : 128 * i + 128] = jnp.where(c == 0, right, left)
        R.w3m[c, :, 128 * i : 128 * i + 128] = jnp.where(c == 0, left, right)
    sib_push(K.w3x, R.w3s, R.w3m.at[c])

    R.modr[p] = R.mods[t]
    R.wf[p, c] = R.wfs[...]
    R.tokh[p] = R.tok[t]
    R.wqkv[p, c] = R.wqs[x]
    R.path[p] = R.pat[t]
    R.go2[c, t] = R.go[t]
    R.camr[b] = R.cam[...]

    got(K.mod, R.modr.at[0:7])
    near_push(K.w2, lambda xx, tt: R.wfs, R.wf.at[p, c], R.wf.at[0:7, 0])
    spread_first(K.w1a, K.w1b, R.wks, R.wk)
    R.modo[...] = jnp.sum(R.modr[...], 0)
    sib_push(K.modx, R.modo, R.modx)

    got(K.wq, R.wqkv.at[0:7, 0])
    sib_push(K.wqx, R.wqkv.at[:, c], R.wqkv.at[:, c])

    got(K.tok, R.tokh.at[0:7])

    def norm_step(i, carry):
        R.n1h[i] = normalize(R.tokh[pl.ds(2 * i, 2)].reshape(128, 512).astype(F32))[0]
        return carry

    lax.fori_loop(0, 4, norm_step, 0)

    got(K.modx, R.modx)
    modv = R.modo[...] + R.modx[...]
    scale_up = 1.0 + jnp.concatenate([modv[i : i + 1, :] for i in range(4)], 1)
    shift = jnp.concatenate([modv[i : i + 1, :] for i in range(4, 8)], 1)
    got(K.wqx, R.wqkv.at[:, 0])

    def qkv_step(i, carry):
        a1 = (R.n1h[i] * scale_up + shift).astype(BF)
        R.a1h[i] = a1
        qkv = dot(a1, R.wqkv[...].reshape(512, 384))
        R.qs[i] = (qkv[:, 0:128].astype(BF).astype(F32) * 0.125).astype(BF)
        R.kv[c, i] = qkv[:, 128:384].astype(BF)
        return carry

    spread_second(K.w1a, K.w1b, K.w1c, R.wk)
    lax.fori_loop(0, 4, qkv_step, 0)
    sib_push(K.kv, R.kv.at[c], R.kv.at[c])
    near_push(K.pat, lambda xx, tt: R.pat.at[tt], R.path.at[p], R.path.at[0:7])
    push(K.go, R.go.at[1 - t], R.go2.at[c, t], partner)
    later(K.go, R.go.at[0])

    def cam_step(n, carry):
        pltpu.make_async_remote_copy(
            src_ref=R.cam,
            dst_ref=R.camr.at[b],
            send_sem=ss.at[K.cam],
            recv_sem=rs.at[K.cam],
            device_id=did((b + n) % 8, x, t, c),
            device_id_type=MESH,
        ).start()
        return carry
    lax.fori_loop(1, 8, cam_step, 0)
    later(K.cam, R.camr.at[0:7])

    eye = jnp.where(iota((128, 128), 0) == iota((128, 128), 1), 1.0, 0.0).astype(BF)
    mask0 = jnp.where(iota((1, 128), 1) < 64, 1.0, 0.0).astype(BF)
    mask1 = jnp.where(iota((1, 128), 1) < 64, 0.0, 1.0).astype(BF)

    def transposed(rows):
        return dot_nt(eye, rows).astype(BF)

    def two_heads(rows):
        return jnp.concatenate([rows * mask0, rows * mask1], 0)

    def unfold(columns):
        return jnp.concatenate([columns[0:64, 0:128], columns[64:128, 128:256]], 0).T

    def attend(queries, keys, values_t, off):
        scores = dot_nt(keys, two_heads(queries))
        if off is not None:
            scores = scores + jnp.concatenate([off, off], 1)
        raised = jnp.exp(scores - jnp.max(scores, 0, keepdims=True))
        weights = (raised * (1.0 / jnp.sum(raised, 0, keepdims=True))).astype(BF)
        return weights, unfold(dot(values_t, weights)).astype(BF)

    def attend_back(queries, douts, keys_t, values, weights_low):
        q, dout = two_heads(queries), two_heads(douts)
        weights = weights_low.astype(F32)
        dweights = dot_nt(values, dout)
        delta = jnp.sum(weights * dweights, 0, keepdims=True)
        dscores = (weights * (dweights - delta)).astype(BF)
        dquery = (unfold(dot(keys_t, dscores)) * 0.125).astype(BF)
        return dquery, dot(dscores, q), dot(weights_low, dout)

    def own_columns(ref):
        return jnp.concatenate([ref[i] for i in range(4)], 1)

    got(K.kv, R.kv.at[0])

    def self_keys():
        return R.kv[:, :, :, 0:128].reshape(1024, 128)

    def self_values():
        return R.kv[:, :, :, 128:256].reshape(1024, 128)

    R.kt[...] = transposed(self_keys())
    R.vt[...] = transposed(self_values())

    def self_step(n, carry):
        xc = (x + 2 + 3 * n + (n // 2) * (7 - 2 * n)) % 4
        weights, out = attend(R.qs[xc], self_keys(), R.vt[...], None)
        R.p1[xc] = weights
        R.o1s[xc] = out

        @pl.when(n < 3)
        def _():
            push(K.o1, R.o1s.at[xc], R.o1r.at[x], did(b, xc, t, c))

        return carry

    lax.fori_loop(0, 4, self_step, 0)
    later(K.o1, R.o1r.at[0:3])
    R.o1r[x] = R.o1s[x]

    got(K.w2, R.wf.at[0:7, 0])
    spread_last(K.w2d, R.wf)
    spread_first(K.w4a, K.w4b, R.w_down, R.w4)
    got(K.w3x, R.w3s)
    R.w3[p] = R.w3m[...]
    near_push(K.w3, lambda xx, tt: R.w3m, R.w3.at[p], R.w3.at[0:7])
    spread_third(K.w1c, R.wk)
    spread_last(K.w1d, R.wk)
    got(K.go, R.go2.at[0, 0])
    sib_push(K.gox, R.go2.at[c], R.go2.at[c])

    live = R.counts[t]
    for cc in range(2):
        for pp in range(8):
            slots = iota((80, 128), 0) + 80 * (2 * pp + cc)
            R.bias[640 * cc + 80 * pp : 640 * cc + 80 * pp + 80, :] = jnp.where(slots < live, 0.0, BIG_NEG)

    def w_out():
        return R.wf[:, :, :, 0:512].reshape(512, 512)

    def c_query():
        return R.wf[:, :, :, 512:1024].reshape(512, 512)

    def c_out():
        return R.wf[:, :, :, 1024:1536].reshape(512, 512)

    def c_pair():
        return R.wk[:, :, :, 0:1024].reshape(512, 1024)

    def spread_rows():
        f = iota((384, 512), 0)
        return jnp.where(iota((384, 512), 1) == f + (f * 21846) // 65536, 1.0, 0.0).astype(BF)

    got(K.w1d, R.wk.at[:, 0])
    R.wp[...] = dot(spread_rows(), R.wk[:, :, :, 1024:1536].reshape(512, 512)).astype(BF)
    got(K.pat, R.path.at[0:7])

    def patch_step(i, carry):
        projected = dot(R.path[pl.ds(2 * i, 2)].reshape(160, 384), R.wp[...]).astype(BF)
        R.pp[i] = projected
        R.kvc[c, i] = dot(projected, c_pair()).astype(BF)
        return carry

    lax.fori_loop(0, 4, patch_step, 0)
    sib_push(K.kvc, R.kvc.at[c], R.kvc.at[c])

    got(K.w2d, R.wf.at[:, 0])
    packed = R.wf[:, :, :, 1536:1664].reshape(512, 128)
    pick = jnp.where(iota((16, 512), 1) == 32 * iota((16, 512), 0), 1.0, 0.0).astype(BF)
    vectors = dot(pick, packed).astype(BF)
    for v in range(4):
        spread = jnp.where(iota((128, 512), 0) == 32 * v + iota((128, 512), 1) % 32, 1.0, 0.0).astype(BF)
        placed = jnp.where(iota((16, 512), 1) // 32 == iota((16, 512), 0), dot(vectors, spread), 0.0)
        R.gv[v : v + 1, :] = column_sum(placed)

    x_got(K.o1, R.o1r)
    x1 = R.tokh[pl.ds(2 * x, 2)].reshape(128, 512).astype(F32) + dot(own_columns(R.o1r), w_out())
    R.x1[...] = x1
    n2, i2 = normalize(x1)
    R.n2[...] = n2
    R.i2[...] = jnp.broadcast_to(i2, (128, 128))
    a2 = (n2 * R.gv[0:1, :] + R.gv[1:2, :]).astype(BF)
    R.a2[...] = a2
    qc = (dot(a2, c_query()).astype(BF).astype(F32) * 0.125).astype(BF)
    for i in range(4):
        R.qc[i] = qc[:, 128 * i : 128 * i + 128]

    spread_second(K.w4a, K.w4b, K.w4c, R.w4)

    got(K.kvc, R.kvc.at[0])

    def cross_pair(i):
        keys = R.kvc[:, :, :, pl.ds(pl.multiple_of(128 * i, 128), 128)].reshape(1280, 128)
        values = R.kvc[:, :, :, pl.ds(pl.multiple_of(512 + 128 * i, 128), 128)].reshape(1280, 128)
        return keys, values

    def cross_step(i, carry):
        keys, values = cross_pair(i)
        R.p2[i], R.o2[i] = attend(R.qc[i], keys, transposed(values), R.bias[...])
        return carry

    lax.fori_loop(0, 4, cross_step, 0)
    x2 = R.x1[...] + dot(own_columns(R.o2), c_out())
    R.x2[...] = x2
    n3, i3 = normalize(x2)
    R.n3[...] = n3
    R.i3[...] = jnp.broadcast_to(i3, (128, 128))
    a3 = (n3 * R.gv[2:3, :] + R.gv[3:4, :]).astype(BF)
    R.a32[c] = a3
    sib_push(K.a3, R.a32.at[c], R.a32.at[c])

    got(K.w3, R.w3.at[0:7])
    spread_third(K.w4c, R.w4)
    got(K.gox, R.go2.at[0])

    def w_up():
        return R.w3[...].reshape(512, 1024)

    def w_down():
        return R.w4[...].reshape(1024, 512)

    def perceptron(cc):
        u = dot(R.a32[cc], w_up()).astype(BF).astype(F32)
        dg = dot_nt(R.go2[cc].reshape(128, 512), w_down()).astype(BF).astype(F32)
        th = jnp.tanh(GELU_K * (u + GELU_C * u * u * u))
        R.g2[cc] = (0.5 * u * (1.0 + th)).astype(BF)
        slope = 0.5 * (1.0 + th) + 0.5 * u * (1.0 - th * th) * (GELU_K * (1.0 + 3.0 * GELU_C * u * u))
        du = (dg * slope).astype(BF)
        R.du2[cc] = du
        return dot_nt(du, w_up())

    R.dao[...] = perceptron(c)
    got(K.a3, R.a32.at[0])
    R.das[...] = perceptron(1 - c).astype(BF)
    sib_push(K.da, R.das, R.dar)
    R.ops[...] = dot(R.g2[1 - c], w_down()).astype(BF)
    sib_push(K.op, R.ops, R.opr)
    R.oo[...] = dot(R.g2[c], w_down())

    def pack_rows(read, width, dst):
        def step(n, carry):
            base = 64 * (n // 2) + 8 * (n % 2)
            parts = [read[pl.ds(pl.multiple_of(base + 16 * k, 8), 8), :] for k in range(4)]
            dst[n, :, 0:width] = jnp.concatenate(parts, 0).astype(BF)
            return carry

        lax.fori_loop(0, 16, step, 0)

    R.gus[...] = dot_tn(R.a32[...].reshape(256, 512), R.du2[...].reshape(256, 1024)).astype(BF).reshape(8, 4, 16, 1024)
    x_push(K.ux, lambda xx: R.gus.at[:, xx], R.gur)
    R.gur[x] = R.gus[:, x]
    for i in range(8):
        grad = dot_tn(R.g2[:, :, 128 * i : 128 * i + 128].reshape(256, 128), R.go2[...].reshape(256, 512)).astype(BF)
        for k in range(4):
            R.e1s[2 * i + k % 2, :, 512 * (k // 2) : 512 * (k // 2) + 512] = grad[32 * k : 32 * k + 32]

    plane_push(K.e1, R.e1s, R.e1r)
    R.e1r[i_me] = R.e1s[i_me]

    def sum4(ref):
        return (ref[0].astype(F32) + ref[1].astype(F32)) + (ref[2].astype(F32) + ref[3].astype(F32))

    def put_vector(at, row):
        for i in range(4):
            R.tb[at + i : at + i + 1, :] = row[:, 128 * i : 128 * i + 128]

    def put_halves(own, other, at, grad):
        width = grad.shape[1] // 2
        left, right = grad[:, 0:width], grad[:, width : 2 * width]
        own[:, at : at + width] = jnp.where(c == 0, left, right)
        other[:, at : at + width] = jnp.where(c == 0, right, left).astype(BF)

    got(K.da, R.dar)
    dthird = R.dao[...] + R.dar[...].astype(F32)
    n3 = R.n3[...]
    put_vector(16, column_sum(dthird * n3))
    put_vector(20, column_sum(dthird))
    dy = R.go2[c].reshape(128, 512).astype(F32)
    dx2 = dy + norm_back(dthird * R.gv[2:3, :], n3, R.i3[:, 0:1])
    R.dx2[...] = dx2
    dx2_low = dx2.astype(BF)
    do2 = dot_nt(dx2_low, c_out()).astype(BF)
    for i in range(4):
        R.do2[i] = do2[:, 128 * i : 128 * i + 128]

    def cross_back(i, carry):
        keys, values = cross_pair(i)
        R.dqc[i], dk, dv = attend_back(R.qc[i], R.do2[i], transposed(keys), values, R.p2[i])
        R.dkvc[:, :, :, pl.ds(pl.multiple_of(128 * i, 128), 128)] = dk.astype(BF).reshape(2, 4, 160, 128)
        R.dkvc[:, :, :, pl.ds(pl.multiple_of(512 + 128 * i, 128), 128)] = dv.astype(BF).reshape(2, 4, 160, 128)
        return carry

    lax.fori_loop(0, 4, cross_back, 0)
    sib_push(K.dkc, R.dkvc.at[1 - c], R.dkcr)

    dqc = own_columns(R.dqc)
    dsecond = dot_nt(dqc, c_query())
    n2 = R.n2[...]
    put_vector(8, column_sum(dsecond * n2))
    put_vector(12, column_sum(dsecond))
    dx1 = R.dx2[...] + norm_back(dsecond * R.gv[0:1, :], n2, R.i2[:, 0:1])
    R.dx1[...] = dx1
    dx1_low = dx1.astype(BF)
    do1 = dot_nt(dx1_low, w_out()).astype(BF)
    for i in range(4):
        R.do1s[i] = do1[:, 128 * i : 128 * i + 128]
    for d in (2, 1, 3):
        xx = (x + d) % 4
        push(K.do1, R.do1s.at[xx], R.do1r.at[x], did(b, xx, t, c), slot=do1_base + x)
    later(K.do1, R.do1r.at[0:3])
    R.do1r[x] = R.do1s[x]

    got(K.op, R.opr)
    R.outs[...] = (R.x2[...] + R.oo[...] + R.opr[...].astype(F32)).astype(BF).reshape(2, 64, 512)
    push(K.out, R.outs.at[1 - t], R.out_tok.at[t], partner)
    later(K.out, R.outs.at[0])
    R.out_tok[t] = R.outs[t]

    got(K.dkc, R.dkcr)

    def patch_back(i, carry):
        dkv = (R.dkvc[c, i].astype(F32) + R.dkcr[i].astype(F32)).astype(BF)
        R.dks[i] = dkv
        dpp = dot_nt(dkv, c_pair()).astype(BF)
        R.dpp[i] = dpp
        R.gps[i] = dot_nt(dpp, R.wp[...]).astype(BF)

        @pl.when(i != x)
        def _():
            push(K.gp, R.gps.at[i], R.gpr.at[x], did(b, i, t, c))

        return carry

    lax.fori_loop(0, 4, patch_back, 0)
    later(K.gp, R.gpr.at[0:3])
    R.gpr[x] = R.gps[x]
    grad = dot_tn(R.pp[...].reshape(640, 512), R.dks[...].reshape(640, 1024))
    put_halves(R.ga, R.gas, 0, grad[:, 0:512])
    put_halves(R.ga, R.gas, 256, grad[:, 512:1024])
    spread = dot(R.path[...].reshape(640, 384), spread_rows()).astype(BF)
    put_halves(R.ga, R.gas, 512, dot_tn(spread, R.dpp[...].reshape(640, 512)))
    put_halves(R.ga, R.gas, 768, dot_tn(own_columns(R.o2), R.dx2[...].astype(BF)))
    sib_push(K.ga, R.gas, R.gar)
    put_halves(R.gb2, R.gbs, 0, dot_tn(R.a2[...], dqc))
    put_halves(R.gb2, R.gbs, 256, dot_tn(own_columns(R.o1r), dx1_low))
    sib_push(K.gb, R.gbs, R.gbr)
    x_got(K.ux, R.gur)

    def up_step(n, carry):
        total = (R.gur[0, n].astype(F32) + R.gur[1, n].astype(F32)) + (R.gur[2, n].astype(F32) + R.gur[3, n].astype(F32))
        for k in range(2):
            parts = [total[8 * k : 8 * k + 8, 256 * i : 256 * i + 256] for i in range(4)]
            R.e2s[2 * n + k, :, 1024:1280] = jnp.concatenate(parts, 0).astype(BF)
        return carry

    lax.fori_loop(0, 8, up_step, 0)
    got(K.ga, R.gar)
    R.ga[...] += R.gar[...].astype(F32)
    pack_rows(R.ga, 1024, R.e2s)
    plane_push(K.e2, R.e2s, R.e2r)
    R.e2r[i_me] = R.e2s[i_me]
    got(K.gb, R.gbr)
    R.gb2[...] += R.gbr[...].astype(F32)
    pack_rows(R.gb2, 512, R.e4s)
    plane_push(K.e4, R.e4s, R.e4r)
    R.e4r[i_me] = R.e4s[i_me]

    R.dkv[...] = jnp.zeros(R.dkv.shape, F32)

    def self_back(n, carry):
        xc = (x + 3 * n + (n // 2) * (7 - 2 * n)) % 4

        @pl.when(n > 0)
        def _():
            pltpu.make_async_copy(R.do1r.at[0], R.do1r.at[0], rs.at[do1_base + xc]).wait()

        R.dq[xc], dk, dv = attend_back(R.qs[xc], R.do1r[xc], R.kt[...], self_values(), R.p1[xc])
        R.dkv[:, :, 0:128] += dk.reshape(2, 512, 128)
        R.dkv[:, :, 128:256] += dv.reshape(2, 512, 128)
        return carry

    lax.fori_loop(0, 4, self_back, 0)
    R.dkvs[...] = R.dkv[1 - c].astype(BF)
    sib_push(K.dkv, R.dkvs, R.dkvr)
    got(K.dkv, R.dkvr)
    R.dqkv[:, 0:128] = R.dq[...].reshape(512, 128)
    R.dqkv[:, 128:384] = (R.dkv[c] + R.dkvr[...].astype(F32)).astype(BF)

    R.gc[...] = dot_tn(R.a1h[...].reshape(512, 512), R.dqkv[...])
    pack_rows(R.gc, 384, R.e3s)
    plane_push(K.e3, R.e3s, R.e3r)
    R.e3r[i_me] = R.e3s[i_me]

    def first_step(i, sums):
        d1 = dot_nt(R.dqkv[pl.ds(pl.multiple_of(128 * i, 128), 128), :], R.wqkv[...].reshape(512, 384))
        R.d1s[i] = d1.astype(BF)

        @pl.when(i != x)
        def _():
            push(K.d1, R.d1s.at[i], R.d1r.at[x], did(b, i, t, c))

        return sums[0] + column_sum(d1 * R.n1h[i]), sums[1] + column_sum(d1)

    zero = jnp.zeros((1, 512), F32)
    dscale, dshift = lax.fori_loop(0, 4, first_step, (zero, zero))
    later(K.d1, R.d1r.at[0:3])
    R.d1r[x] = R.d1s[x]
    put_vector(0, dscale)
    put_vector(4, dshift)
    sib_push(K.tbs, R.tb, R.tbs)
    got(K.tbs, R.tbs)
    R.tbx[...] = R.tb[...] + R.tbs[...]
    x_push(K.tbx, lambda xx: R.tbx, R.tbr)
    R.tbr[x] = R.tbx[...]

    x_got(K.tbx, R.tbr)
    R.tbo[...] = (R.tbr[0] + R.tbr[1]) + (R.tbr[2] + R.tbr[3])
    plane_push(K.tbp, R.tbo, R.tbp)
    R.tbp[i_me] = R.tbo[...]

    x_got(K.d1, R.d1r)
    dfirst = sum4(R.d1r)
    n1, i1 = normalize(R.tokh[pl.ds(2 * x, 2)].reshape(128, 512).astype(F32))
    dstream = R.dx1[...] + norm_back(dfirst * scale_up, n1, i1)
    R.gts[...] = dstream.astype(BF).reshape(2, 64, 512)
    push(K.gt, R.gts.at[1 - t], R.g_tok.at[t], partner)
    later(K.gt, R.gts.at[0])
    R.g_tok[t] = R.gts[t]

    x_got(K.gp, R.gpr)
    R.gpo[...] = sum4(R.gpr).astype(BF).reshape(2, 80, 384)
    push(K.gpz, R.gpo.at[1 - t], R.g_pat.at[t], partner)
    later(K.gpz, R.gpo.at[0])
    R.g_pat[t] = R.gpo[t]

    def rows_of(ref):
        return lambda xx: ref.at[pl.ds(pl.multiple_of(8 * xx, 8), 8)]

    def to_owners(name, src, dst):
        x_push(name, rows_of(src), dst)
        dst[x] = src[pl.ds(pl.multiple_of(8 * x, 8), 8), :]

    got(K.e3, R.e3r.at[0:15])
    R.u3s[...] = plane_sum(R.e3r)
    to_owners(K.u3, R.u3s, R.u3r)

    got(K.e1, R.e1r.at[0:15])
    total = plane_sum(R.e1r)
    R.dns[0] = total[:, 0:512]
    R.dns[1] = total[:, 512:1024]
    for k in range(2):
        owner = 2 * c + k

        @pl.when(x != owner)
        def _():
            push((K.dn0, K.dn1)[k], R.dns.at[k], R.dnr.at[x], did(b, owner, t, c), slot=K.dnr)

        later((K.dn0, K.dn1)[k], R.dns.at[k], x != owner)

        @pl.when(x == owner)
        def _():
            R.dnr[x] = R.dns[k]

    got(K.e2, R.e2r.at[0:15])
    total = plane_sum(R.e2r)
    R.u2s[:, 0:1024] = total[:, 0:1024]
    for i in range(4):
        R.u1o[:, 256 * i : 256 * i + 256] = total[8 * i : 8 * i + 8, 1024:1280]
    sib_push(K.u1z, R.u1o, R.u1z)
    got(K.e4, R.e4r.at[0:15])
    R.u2s[:, 1024:1536] = plane_sum(R.e4r)
    to_owners(K.u2, R.u2s, R.u2r)

    x_got(K.u3, R.u3r)
    sib_push(K.u3z, R.u3r, R.u3z)

    @pl.when(x // 2 == c)
    def _():
        x_got(K.dnr, R.dnr)
        R.dno[...] = (R.dnr[0] + R.dnr[1]) + (R.dnr[2] + R.dnr[3])
        push(K.dnz, R.dno.at[pl.ds(pl.multiple_of(16 - 16 * c, 16), 16)], R.dnz, sibling)

    later(K.dnz, R.dnz, x // 2 == c)
    x_got(K.u2, R.u2r)

    R.u2o[...] = (R.u2r[0] + R.u2r[1]) + (R.u2r[2] + R.u2r[3])
    sib_push(K.u2z, R.u2o, R.u2z)

    got(K.cam, R.camr.at[0:7])
    got(K.tbp, R.tbp.at[0:15])
    wanted = iota((8, 128), 1) == 8 * j + iota((8, 128), 0)
    acc = [jnp.zeros((8, 128), F32) for _ in range(8)]
    vec = jnp.zeros((16, 128), F32)
    for o in range(16):
        row = R.camr[o // 2, pl.ds(8 * (o % 2) + b, 1), :]
        weight = jnp.sum(jnp.where(wanted, row, 0.0), 1, keepdims=True)
        dmod = R.tbp[o, 0:8, :]
        for i in range(8):
            acc[i] = acc[i] + weight * dmod[i : i + 1, :]
        vec = vec + R.tbp[o, 8:24, :]
    for i in range(8):
        R.g_mod[:, 128 * i : 128 * i + 128] = acc[i]
    for v in range(4):
        for i in range(4):
            R.g_vec[v : v + 1, 128 * i : 128 * i + 128] = vec[4 * v + i : 4 * v + i + 1, :]

    def mine(v):
        return jnp.where(c == 0, v[0:4], v[4:8])

    def halves(own, other):
        return jnp.where(c == 0, own, other), jnp.where(c == 0, other, own)

    got(K.u3z, R.u3z)
    for k in range(4):
        total = mine(R.u3r[k] + R.u3z[k])
        for n, ref in enumerate((R.g_query, R.g_key, R.g_value)):
            ref[:, 128 * k : 128 * k + 128] = total[:, 128 * n : 128 * n + 128]
    got(K.u1z, R.u1z)
    for n, part in enumerate(halves(mine(R.u1o[...]), mine(R.u1z[...]))):
        for i in range(8):
            R.g_up[:, 256 * i + 128 * n : 256 * i + 128 * n + 128] = part[:, 128 * i : 128 * i + 128]

    @pl.when(x // 2 == c)
    def _():
        R.g_down[...] = R.dno[pl.ds(pl.multiple_of(16 * c, 16), 16), :]

    @pl.when(x // 2 != c)
    def _():
        got(K.dnz, R.dnz)
        R.g_down[...] = R.dnz[...]

    got(K.u2z, R.u2z)
    for n, part in enumerate(halves(mine(R.u2o[...]), mine(R.u2z[...]))):
        for k, ref in enumerate((R.g_ckey, R.g_cvalue, R.g_patch, R.g_cout, R.g_cquery, R.g_out)):
            rows = ref.shape[0]
            ref[:, 256 * n : 256 * n + 256] = part[0:rows, 256 * k : 256 * k + 256]

    got(K.out, R.outs.at[0])
    got(K.gt, R.gts.at[0])
    got(K.gpz, R.gpo.at[0])
    for name, like, when in pending:
        if when is None:
            sent(name, like)
        else:
            pl.when(when)(functools.partial(sent, name, like))


def copies(*refs):
    for source, target in zip(refs[: len(OUTPUTS)], refs[len(OUTPUTS) :]):
        target[...] = source[...]


def hand_over(arrays):
    spec = pl.BlockSpec(memory_space=pltpu.VMEM)
    return pl.pallas_call(
        copies,
        out_shape=[jax.ShapeDtypeStruct(s, d) for s, d in OUTPUTS.values()],
        in_specs=[spec] * len(OUTPUTS),
        out_specs=[spec] * len(OUTPUTS),
        name="results",
    )(*arrays)


def on_device(
    tokens, patches, camera, counts, grad_out, w_mod, w_query, w_key, w_value, w_out, w_patch,
    c_query, c_key, c_value, c_out, gain_two, bias_two, gain_three, bias_three, w_up, w_down,
):
    vectors = jnp.concatenate([gain_two, bias_two, gain_three, bias_three]).reshape(1, 128)
    gb = jnp.broadcast_to(vectors, (32, 128))
    vmem = pl.BlockSpec(memory_space=pltpu.VMEM)
    outs = pl.pallas_call(
        kernel,
        out_shape=[jax.ShapeDtypeStruct(s, d) for s, d in OUTPUTS.values()],
        in_specs=[pl.BlockSpec(memory_space=space) for space in INPUTS.values()],
        out_specs=[vmem] * len(OUTPUTS),
        scratch_shapes=[pltpu.VMEM(s, d) for s, d in SCRATCH.values()]
        + [pltpu.SemaphoreType.DMA((len(K),)), pltpu.SemaphoreType.DMA((len(K) + 4,))],
        compiler_params=pltpu.CompilerParams(
            collective_id=0, has_side_effects=True, vmem_limit_bytes=58 << 20
        ),
        name="layer",
    )(
        tokens, patches, camera, counts, grad_out, w_mod, w_query, w_key, w_value, w_out,
        w_patch, c_query, c_key, c_value, c_out, gb, w_up, w_down,
    )
    *outs, vecs = hand_over(outs)
    at = 64 * lax.axis_index("batch") + 4 * lax.axis_index("blk")
    vecs = lax.dynamic_slice(vecs, (0, at), (4, 4))
    return (*outs[:13], vecs[0], vecs[1], vecs[2], vecs[3], *outs[13:])


def solution(mesh):
    weight = P("blk", None)
    whole = P(("batch", "blk"), None)
    vector = P(("batch", "blk"))
    rows = P("batch", "blk", None)
    return jax.shard_map(
        on_device,
        mesh=mesh,
        in_specs=(
            rows, rows, P("batch", None), P("batch"), rows,
            *(weight,) * 10, *(P("blk"),) * 4, weight, weight,
        ),
        out_specs=(rows, rows, rows, *(whole,) * 10, *(vector,) * 4, whole, whole),
        check_vma=False,
    )
```

```python
import enum
import functools
import types

import jax
import jax.numpy as jnp
from jax import lax
from jax.experimental import pallas as pl
from jax.experimental.pallas import tpu as pltpu
from jax.sharding import PartitionSpec as P

F32 = jnp.float32
BF = jnp.bfloat16
MESH = pl.DeviceIdType.MESH
EPSILON = 1e-05
BIG_NEG = -1e30
GELU_K = 0.7978845608028654
GELU_C = 0.044715


def dot(left, right):
    return jnp.dot(left, right, preferred_element_type=F32)


def dot_nt(left, right):
    return lax.dot_general(left, right, (((1,), (1,)), ((), ())), preferred_element_type=F32)


def dot_tn(left, right):
    return lax.dot_general(left, right, (((0,), (0,)), ((), ())), preferred_element_type=F32)


def normalize(stream):
    centred = stream - jnp.mean(stream, -1, keepdims=True)
    inverse = lax.rsqrt(jnp.mean(centred * centred, -1, keepdims=True) + EPSILON)
    return centred * inverse, inverse


def norm_back(dnormed, normed, inverse):
    return inverse * (
        dnormed
        - jnp.mean(dnormed, -1, keepdims=True)
        - normed * jnp.mean(dnormed * normed, -1, keepdims=True)
    )


def column_sum(rows):
    return jnp.sum(rows, 0, keepdims=True)


def iota(shape, dim):
    return lax.broadcasted_iota(jnp.int32, shape, dim)


class Inputs:
    tok = pltpu.VMEM
    pat = pltpu.VMEM
    camera = pltpu.VMEM
    counts = pltpu.SMEM
    go = pltpu.VMEM
    w_mod = pltpu.VMEM
    w_query = pltpu.VMEM
    w_key = pltpu.VMEM
    w_value = pltpu.VMEM
    w_out = pltpu.VMEM
    w_patch = pltpu.VMEM
    c_query = pltpu.VMEM
    c_key = pltpu.VMEM
    c_value = pltpu.VMEM
    c_out = pltpu.VMEM
    gain_two = pltpu.VMEM
    bias_two = pltpu.VMEM
    gain_three = pltpu.VMEM
    bias_three = pltpu.VMEM
    w_up = pltpu.VMEM
    w_down = pltpu.VMEM


class Outputs:
    out_tok = ((2, 64, 512), BF)
    g_tok = ((2, 64, 512), BF)
    g_pat = ((2, 80, 384), BF)
    g_mod = ((8, 1024), F32)
    g_query = ((4, 512), F32)
    g_key = ((4, 512), F32)
    g_value = ((4, 512), F32)
    g_out = ((4, 512), F32)
    g_patch = ((3, 512), F32)
    g_cquery = ((4, 512), F32)
    g_ckey = ((4, 512), F32)
    g_cvalue = ((4, 512), F32)
    g_cout = ((4, 512), F32)
    g_up = ((4, 2048), F32)
    g_down = ((16, 512), F32)
    g_vec = ((4, 512), F32)


class Scratch:
    cam = ((16, 128), F32)
    tokh = ((8, 64, 512), BF)
    path = ((8, 80, 384), BF)
    wqs = ((4, 32, 384), BF)
    wfs = ((32, 1152), BF)
    wqkv = ((8, 2, 32, 384), BF)
    wf = ((8, 2, 32, 1152), BF)
    mods = ((2, 8, 128), F32)
    modr = ((8, 8, 128), F32)
    modo = ((8, 128), F32)
    modx = ((8, 128), F32)
    camr = ((8, 16, 128), F32)
    gv = ((8, 512), F32)
    bias = ((1280, 128), F32)
    n1h = ((4, 128, 512), F32)
    a1h = ((4, 128, 512), BF)
    qs = ((4, 128, 128), BF)
    kv = ((2, 4, 128, 256), BF)
    p1 = ((4, 1024, 256), BF)
    o1s = ((4, 128, 128), BF)
    o1r = ((4, 128, 128), BF)
    x1 = ((128, 512), F32)
    n2 = ((128, 512), F32)
    i2 = ((128, 128), F32)
    a2 = ((128, 512), BF)
    wk = ((8, 2, 32, 1536), BF)
    kvc = ((2, 4, 160, 1024), BF)
    p2 = ((4, 1280, 256), BF)
    x2 = ((128, 512), F32)
    n3 = ((128, 512), F32)
    i3 = ((128, 128), F32)
    das = ((128, 512), BF)
    dar = ((128, 512), BF)
    ops = ((128, 512), BF)
    opr = ((128, 512), BF)
    outs = ((2, 64, 512), BF)
    dx2 = ((128, 512), F32)
    dkvc = ((2, 4, 160, 1024), BF)
    dkcr = ((4, 160, 1024), BF)
    gps = ((4, 160, 384), BF)
    gpr = ((4, 160, 384), BF)
    gpo = ((2, 80, 384), BF)
    dx1 = ((128, 512), F32)
    do1s = ((4, 128, 128), BF)
    do1r = ((4, 128, 128), BF)
    dkv = ((2, 512, 256), F32)
    dkvs = ((512, 256), BF)
    dkvr = ((512, 256), BF)
    dqkv = ((512, 384), BF)
    d1s = ((4, 128, 512), BF)
    d1r = ((4, 128, 512), BF)
    gts = ((2, 64, 512), BF)
    dq = ((4, 128, 128), BF)
    gb2 = ((512, 512), F32)
    gbs = ((512, 512), BF)
    gbr = ((512, 512), BF)
    gc = ((512, 384), F32)
    e1s = ((16, 32, 1024), BF)
    e1r = ((16, 32, 1024), BF)
    e2s = ((16, 32, 512), BF)
    e2r = ((16, 32, 512), BF)
    e3s = ((16, 32, 384), BF)
    e3r = ((16, 32, 384), BF)
    u1o = ((8, 1536), F32)
    u1z = ((8, 1536), F32)
    dns = ((2, 32, 512), F32)
    dnr = ((4, 32, 512), F32)
    dnz = ((16, 512), F32)
    u2s = ((32, 1024), F32)
    u2r = ((4, 8, 1024), F32)
    u2o = ((8, 1024), F32)
    u2z = ((8, 1024), F32)
    u3s = ((32, 384), F32)
    u3r = ((4, 8, 384), F32)
    u3z = ((4, 8, 384), F32)
    tb = ((24, 128), F32)
    tbs = ((24, 128), F32)
    tbx = ((24, 128), F32)
    tbr = ((4, 24, 128), F32)
    tbo = ((24, 128), F32)
    tbp = ((16, 24, 128), F32)
    wks = ((32, 1536), BF)
    kt = ((128, 1024), BF)
    vt = ((128, 1024), BF)
    wp = ((384, 512), BF)
    pp = ((4, 160, 512), BF)
    qc = ((4, 128, 128), BF)
    o2 = ((4, 128, 128), BF)
    do2 = ((4, 128, 128), BF)
    dqc = ((4, 128, 128), BF)
    dks = ((4, 160, 1024), BF)
    dpp = ((4, 160, 512), BF)
    w3s = ((32, 1024), BF)
    w3m = ((2, 32, 1024), BF)
    w3 = ((8, 2, 32, 1024), BF)
    w4 = ((8, 128, 512), BF)
    go2 = ((2, 2, 64, 512), BF)
    a32 = ((2, 128, 512), BF)
    g2 = ((2, 128, 1024), BF)
    du2 = ((2, 128, 1024), BF)
    dao = ((128, 512), F32)
    oo = ((128, 512), F32)
    dno = ((32, 512), F32)
    gus = ((8, 4, 16, 1024), BF)
    gur = ((4, 8, 16, 1024), BF)
    ga = ((512, 1024), F32)
    gas = ((512, 1024), BF)
    gar = ((512, 1024), BF)
    e4s = ((16, 32, 512), BF)
    e4r = ((16, 32, 512), BF)
    co = ((8, 2, 32, 512), BF)
    kxs = ((8, 4, 16, 512), BF)
    kxr = ((4, 8, 16, 512), BF)
    e5s = ((16, 32, 384), BF)
    e5r = ((16, 32, 384), BF)


def members(group):
    return {name: value for name, value in vars(group).items() if not name.startswith("_")}


INPUTS, OUTPUTS, SCRATCH = members(Inputs), members(Outputs), members(Scratch)


class K(enum.IntEnum):
    a3 = 0
    cam = 1
    d1 = 2
    da = 3
    dkc = 4
    dkv = 5
    dn0 = 6
    dn1 = 7
    dnr = 8
    dnz = 9
    do1 = 10
    e1 = 11
    e2 = 12
    e3 = 13
    e4 = 14
    e5 = 15
    ga = 16
    gb = 17
    go = 18
    gox = 19
    gp = 20
    gpz = 21
    gt = 22
    kv = 23
    kvc = 24
    kx = 25
    mod = 26
    modx = 27
    o1 = 28
    op = 29
    out = 30
    pat = 31
    tbp = 32
    tbs = 33
    tbx = 34
    tok = 35
    u1z = 36
    u2 = 37
    u2z = 38
    u3 = 39
    u3z = 40
    ux = 41
    w1a = 42
    w1b = 43
    w1c = 44
    w1d = 45
    w2 = 46
    w2d = 47
    w3 = 48
    w3x = 49
    w4a = 50
    w4b = 51
    w4c = 52
    w5 = 53
    w5d = 54
    wq = 55
    wqx = 56


def kernel(*refs):
    *buffers, ss, rs = refs
    R = types.SimpleNamespace(**dict(zip((*INPUTS, *OUTPUTS, *SCRATCH), buffers)))
    b = lax.axis_index("batch")
    j = lax.axis_index("blk")
    x = j // 4
    t = (j // 2) % 2
    c = j % 2
    p = 2 * x + t
    i_me = 2 * b + t

    def did(bb, xx, tt, cc):
        return (bb, xx * 4 + tt * 2 + cc)

    pending = []
    do1_base = len(K)

    def push(name, src, dst, dev, slot=None):
        pltpu.make_async_remote_copy(
            src_ref=src,
            dst_ref=dst,
            send_sem=ss.at[name],
            recv_sem=rs.at[name if slot is None else slot],
            device_id=dev,
            device_id_type=MESH,
        ).start()

    def got(name, like):
        pltpu.make_async_copy(like, like, rs.at[name]).wait()

    def sent(name, like):
        pltpu.make_async_copy(like, like, ss.at[name]).wait()

    def later(name, like, when=None):
        pending.append((name, like, when))

    sibling = did(b, x, t, 1 - c)
    partner = did(b, x, 1 - t, c)
    near = [((x + dx) % 4, (t + dt) % 2) for dx, dt in ((0, 1), (1, 0), (3, 0), (2, 0), (1, 1), (3, 1), (2, 1))]

    def near_push(name, src_of, dst, like):
        for xx, tt in near:
            push(name, src_of(xx, tt), dst, did(b, xx, tt, c))
        later(name, like)

    def x_push(name, src_of, dst_ref):
        for d in (1, 3, 2):
            xx = (x + d) % 4
            push(name, src_of(xx), dst_ref.at[x], did(b, xx, t, c))
        later(name, dst_ref.at[0:3])

    def x_got(name, dst_ref):
        got(name, dst_ref.at[0:3])

    def sib_push(name, src, dst):
        push(name, src, dst, sibling)
        later(name, dst)

    def plane_push(name, src, dst):
        def step(n, carry):
            bb = (b + n // 2) % 8
            tt = (t + n % 2) % 2
            pltpu.make_async_remote_copy(
                src_ref=src.at[2 * bb + tt] if src.shape[0] == 16 else src,
                dst_ref=dst.at[i_me],
                send_sem=ss.at[name],
                recv_sem=rs.at[name],
                device_id=did(bb, x, tt, c),
                device_id_type=MESH,
            ).start()
            return carry

        lax.fori_loop(1, 16, step, 0)
        later(name, dst.at[0:15])

    def plane_sum(ref):
        def step(n, acc):
            return acc + ref[n].astype(F32)

        return lax.fori_loop(1, 16, step, ref[0].astype(F32))

    for i in range(4):
        cols = slice(128 * i, 128 * i + 128)
        R.wqs[i, :, 0:128] = R.w_query[:, cols]
        R.wqs[i, :, 128:256] = R.w_key[:, cols]
        R.wqs[i, :, 256:384] = R.w_value[:, cols]
    lanes = iota((1, 128), 1)
    half = jnp.where(lanes // 64 == c, 1.0, 0.0).astype(F32)
    for o in range(2):
        for i in range(8):
            R.cam[8 * o + i : 8 * o + i + 1, :] = R.camera[o : o + 1, 128 * i : 128 * i + 128].astype(F32)
    row0 = R.cam[pl.ds(j // 2, 1), :] * half
    row1 = R.cam[pl.ds(8 + j // 2, 1), :] * half
    rows = jnp.concatenate([row0, row1, jnp.zeros((14, 128), F32)], 0).astype(BF)
    w_mod = R.w_mod[...]
    modp = dot(rows, jnp.concatenate([w_mod, w_mod], 0))
    for i in range(8):
        R.mods[0, i : i + 1, :] = modp[0:1, 128 * i : 128 * i + 128]
        R.mods[1, i : i + 1, :] = modp[1:2, 128 * i : 128 * i + 128]

    bar = pltpu.get_barrier_semaphore()

    def greet(dev):
        pl.semaphore_signal(bar, inc=1, device_id=dev, device_id_type=MESH)

    for xx, tt in near:
        greet(did(b, xx, tt, c))
    greet(sibling)

    def greet_plane(n, carry):
        greet(did((b + n // 2) % 8, x, (t + n % 2) % 2, c))
        return carry

    lax.fori_loop(1, 16, greet_plane, 0)

    pl.semaphore_wait(bar, 7 + 1 + 15)

    near_push(K.mod, lambda xx, tt: R.mods.at[tt], R.modr.at[p], R.modr.at[0:7])
    near_push(K.tok, lambda xx, tt: R.tok.at[tt], R.tokh.at[p], R.tokh.at[0:7])
    near_push(K.wq, lambda xx, tt: R.wqs.at[xx], R.wqkv.at[p, c], R.wqkv.at[0:7, 0])

    y = b % 4
    xs = (x + y) % 4
    xd = (x + 4 - y) % 4

    def spread_first(same, cross, src, whole):
        push(cross, src, slot(whole, p), did(b, xd, 1 - t, c))
        later(cross, src)

        @pl.when(y > 0)
        def _():
            push(same, src, slot(whole, p), did(b, xd, t, c))

        later(same, src, y > 0)

        @pl.when(y == 0)
        def _():
            slot(whole, p)[...] = src[...]

    def spread_second(same, cross, name, whole):
        got(cross, slot(whole, 0))

        @pl.when(y > 0)
        def _():
            got(same, slot(whole, 0))

        held = slot(whole, pl.ds(2 * xs, 2))
        for d in (2, 1, 3):
            push(name, held, held, did(b - y + (y + d) % 4, x, t, c))
        later(name, slot(whole, slice(0, 6)))

    def slot(whole, at):
        return whole.at[at, c] if len(whole.shape) == 4 else whole.at[at]

    def spread_third(name, whole):
        got(name, slot(whole, slice(0, 6)))

    def spread_last(name, whole):
        sib_push(name, whole.at[:, c], whole.at[:, c])

    f = iota((32, 24), 1)
    apart = jnp.where(iota((32, 24), 0) == f + (f * 21846) // 65536, 1.0, 0.0).astype(BF)
    R.wks[:, 0:512] = R.c_key[...]
    R.wks[:, 512:1024] = R.c_value[...]
    R.wks[:, 1024:1536] = dot(apart, R.w_patch[...]).astype(BF)
    R.wfs[:, 0:512] = R.w_out[...]
    R.wfs[:, 512:1024] = R.c_query[...]
    row = jnp.zeros((1, 128), F32)
    for v, ref in enumerate((R.gain_two, R.bias_two, R.gain_three, R.bias_three)):
        place = jnp.where(iota((32, 128), 1) == 32 * v + iota((32, 128), 0), 1.0, 0.0).astype(BF)
        row = row + dot(ref[...].reshape(1, 32), place)
    R.wfs[:, 1024:1152] = jnp.broadcast_to(row, (32, 128)).astype(BF)
    for i in range(8):
        left, right = R.w_up[:, 256 * i : 256 * i + 128], R.w_up[:, 256 * i + 128 : 256 * i + 256]
        R.w3s[:, 128 * i : 128 * i + 128] = jnp.where(c == 0, right, left)
        R.w3m[c, :, 128 * i : 128 * i + 128] = jnp.where(c == 0, left, right)
    sib_push(K.w3x, R.w3s, R.w3m.at[c])

    R.modr[p] = R.mods[t]
    R.wf[p, c] = R.wfs[...]
    R.co[p, c] = R.c_out[...]
    R.tokh[p] = R.tok[t]
    R.wqkv[p, c] = R.wqs[x]
    R.path[p] = R.pat[t]
    R.go2[c, t] = R.go[t]
    R.camr[b] = R.cam[...]

    got(K.mod, R.modr.at[0:7])
    near_push(K.w2, lambda xx, tt: R.wfs, R.wf.at[p, c], R.wf.at[0:7, 0])
    spread_first(K.w1a, K.w1b, R.wks, R.wk)
    spread_first(K.w4a, K.w4b, R.w_down, R.w4)
    R.modo[...] = jnp.sum(R.modr[...], 0)
    sib_push(K.modx, R.modo, R.modx)

    got(K.wq, R.wqkv.at[0:7, 0])
    sib_push(K.wqx, R.wqkv.at[:, c], R.wqkv.at[:, c])

    got(K.tok, R.tokh.at[0:7])

    def norm_step(i, carry):
        R.n1h[i] = normalize(R.tokh[pl.ds(2 * i, 2)].reshape(128, 512).astype(F32))[0]
        return carry

    lax.fori_loop(0, 4, norm_step, 0)

    got(K.modx, R.modx)
    modv = R.modo[...] + R.modx[...]
    scale_up = 1.0 + jnp.concatenate([modv[i : i + 1, :] for i in range(4)], 1)
    shift = jnp.concatenate([modv[i : i + 1, :] for i in range(4, 8)], 1)
    got(K.wqx, R.wqkv.at[:, 0])

    def qkv_step(i, carry):
        a1 = (R.n1h[i] * scale_up + shift).astype(BF)
        R.a1h[i] = a1
        qkv = dot(a1, R.wqkv[...].reshape(512, 384))
        R.qs[i] = (qkv[:, 0:128].astype(BF).astype(F32) * 0.125).astype(BF)
        R.kv[c, i] = qkv[:, 128:384].astype(BF)
        return carry

    spread_second(K.w1a, K.w1b, K.w1c, R.wk)
    lax.fori_loop(0, 4, qkv_step, 0)
    sib_push(K.kv, R.kv.at[c], R.kv.at[c])
    near_push(K.pat, lambda xx, tt: R.pat.at[tt], R.path.at[p], R.path.at[0:7])
    near_push(K.w5, lambda xx, tt: R.c_out, R.co.at[p, c], R.co.at[0:7, 0])
    push(K.go, R.go.at[1 - t], R.go2.at[c, t], partner)
    later(K.go, R.go.at[0])

    def cam_step(n, carry):
        pltpu.make_async_remote_copy(
            src_ref=R.cam,
            dst_ref=R.camr.at[b],
            send_sem=ss.at[K.cam],
            recv_sem=rs.at[K.cam],
            device_id=did((b + n) % 8, x, t, c),
            device_id_type=MESH,
        ).start()
        return carry
    lax.fori_loop(1, 8, cam_step, 0)
    later(K.cam, R.camr.at[0:7])

    eye = jnp.where(iota((128, 128), 0) == iota((128, 128), 1), 1.0, 0.0).astype(BF)
    mask0 = jnp.where(iota((1, 128), 1) < 64, 1.0, 0.0).astype(BF)
    mask1 = jnp.where(iota((1, 128), 1) < 64, 0.0, 1.0).astype(BF)

    def transposed(rows):
        return dot_nt(eye, rows).astype(BF)

    def two_heads(rows):
        return jnp.concatenate([rows * mask0, rows * mask1], 0)

    def unfold(columns):
        return jnp.concatenate([columns[0:64, 0:128], columns[64:128, 128:256]], 0).T

    def attend(queries, keys, values_t, off):
        scores = dot_nt(keys, two_heads(queries))
        if off is not None:
            scores = scores + jnp.concatenate([off, off], 1)
        raised = jnp.exp(scores - jnp.max(scores, 0, keepdims=True))
        weights = (raised * (1.0 / jnp.sum(raised, 0, keepdims=True))).astype(BF)
        return weights, unfold(dot(values_t, weights)).astype(BF)

    def attend_back(queries, douts, keys_t, values, weights_low):
        q, dout = two_heads(queries), two_heads(douts)
        weights = weights_low.astype(F32)
        dweights = dot_nt(values, dout)
        delta = jnp.sum(weights * dweights, 0, keepdims=True)
        dscores = (weights * (dweights - delta)).astype(BF)
        dquery = (unfold(dot(keys_t, dscores)) * 0.125).astype(BF)
        return dquery, dot(dscores, q), dot(weights_low, dout)

    def own_columns(ref):
        return jnp.concatenate([ref[i] for i in range(4)], 1)

    got(K.kv, R.kv.at[0])

    def self_keys():
        return R.kv[:, :, :, 0:128].reshape(1024, 128)

    def self_values():
        return R.kv[:, :, :, 128:256].reshape(1024, 128)

    R.kt[...] = transposed(self_keys())
    R.vt[...] = transposed(self_values())

    def self_step(n, carry):
        xc = (x + 2 + 3 * n + (n // 2) * (7 - 2 * n)) % 4
        weights, out = attend(R.qs[xc], self_keys(), R.vt[...], None)
        R.p1[xc] = weights
        R.o1s[xc] = out

        @pl.when(n < 3)
        def _():
            push(K.o1, R.o1s.at[xc], R.o1r.at[x], did(b, xc, t, c))

        return carry

    lax.fori_loop(0, 4, self_step, 0)
    later(K.o1, R.o1r.at[0:3])
    R.o1r[x] = R.o1s[x]

    got(K.w2, R.wf.at[0:7, 0])
    spread_last(K.w2d, R.wf)
    spread_second(K.w4a, K.w4b, K.w4c, R.w4)
    got(K.w3x, R.w3s)
    R.w3[p] = R.w3m[...]
    near_push(K.w3, lambda xx, tt: R.w3m, R.w3.at[p], R.w3.at[0:7])
    spread_third(K.w1c, R.wk)
    spread_last(K.w1d, R.wk)
    got(K.go, R.go2.at[0, 0])
    sib_push(K.gox, R.go2.at[c], R.go2.at[c])

    live = R.counts[t]
    for cc in range(2):
        for pp in range(8):
            slots = iota((80, 128), 0) + 80 * (2 * pp + cc)
            R.bias[640 * cc + 80 * pp : 640 * cc + 80 * pp + 80, :] = jnp.where(slots < live, 0.0, BIG_NEG)

    def w_out():
        return R.wf[:, :, :, 0:512].reshape(512, 512)

    def c_query():
        return R.wf[:, :, :, 512:1024].reshape(512, 512)

    def c_out():
        return R.co[...].reshape(512, 512)

    def c_pair():
        return R.wk[:, :, :, 0:1024].reshape(512, 1024)

    def spread_rows():
        f = iota((384, 512), 0)
        return jnp.where(iota((384, 512), 1) == f + (f * 21846) // 65536, 1.0, 0.0).astype(BF)

    got(K.w1d, R.wk.at[:, 0])
    R.wp[...] = dot(spread_rows(), R.wk[:, :, :, 1024:1536].reshape(512, 512)).astype(BF)
    got(K.pat, R.path.at[0:7])

    def patch_step(i, carry):
        projected = dot(R.path[pl.ds(2 * i, 2)].reshape(160, 384), R.wp[...]).astype(BF)
        R.pp[i] = projected
        R.kvc[c, i] = dot(projected, c_pair()).astype(BF)
        push(K.kvc, R.kvc.at[c, i], R.kvc.at[c, i], sibling)
        return carry

    lax.fori_loop(0, 4, patch_step, 0)
    later(K.kvc, R.kvc.at[0])

    got(K.w2d, R.wf.at[:, 0])
    packed = R.wf[:, :, :, 1024:1152].reshape(512, 128)
    pick = jnp.where(iota((16, 512), 1) == 32 * iota((16, 512), 0), 1.0, 0.0).astype(BF)
    vectors = dot(pick, packed).astype(BF)
    for v in range(4):
        spread = jnp.where(iota((128, 512), 0) == 32 * v + iota((128, 512), 1) % 32, 1.0, 0.0).astype(BF)
        placed = jnp.where(iota((16, 512), 1) // 32 == iota((16, 512), 0), dot(vectors, spread), 0.0)
        R.gv[v : v + 1, :] = column_sum(placed)

    x_got(K.o1, R.o1r)
    x1 = R.tokh[pl.ds(2 * x, 2)].reshape(128, 512).astype(F32) + dot(own_columns(R.o1r), w_out())
    R.x1[...] = x1
    n2, i2 = normalize(x1)
    R.n2[...] = n2
    R.i2[...] = jnp.broadcast_to(i2, (128, 128))
    a2 = (n2 * R.gv[0:1, :] + R.gv[1:2, :]).astype(BF)
    R.a2[...] = a2
    qc = (dot(a2, c_query()).astype(BF).astype(F32) * 0.125).astype(BF)
    for i in range(4):
        R.qc[i] = qc[:, 128 * i : 128 * i + 128]


    got(K.kvc, R.kvc.at[0])

    def cross_pair(i):
        keys = R.kvc[:, :, :, pl.ds(pl.multiple_of(128 * i, 128), 128)].reshape(1280, 128)
        values = R.kvc[:, :, :, pl.ds(pl.multiple_of(512 + 128 * i, 128), 128)].reshape(1280, 128)
        return keys, values

    def cross_step(i, carry):
        keys, values = cross_pair(i)
        R.p2[i], R.o2[i] = attend(R.qc[i], keys, transposed(values), R.bias[...])
        return carry

    lax.fori_loop(0, 4, cross_step, 0)
    got(K.w5, R.co.at[0:7, 0])
    spread_last(K.w5d, R.co)
    got(K.w5d, R.co.at[:, 0])
    x2 = R.x1[...] + dot(own_columns(R.o2), c_out())
    R.x2[...] = x2
    n3, i3 = normalize(x2)
    R.n3[...] = n3
    R.i3[...] = jnp.broadcast_to(i3, (128, 128))
    a3 = (n3 * R.gv[2:3, :] + R.gv[3:4, :]).astype(BF)
    R.a32[c] = a3
    sib_push(K.a3, R.a32.at[c], R.a32.at[c])

    got(K.w3, R.w3.at[0:7])
    spread_third(K.w4c, R.w4)
    got(K.gox, R.go2.at[0])

    def w_up():
        return R.w3[...].reshape(512, 1024)

    def w_down():
        return R.w4[...].reshape(1024, 512)

    def perceptron(cc):
        u = dot(R.a32[cc], w_up()).astype(BF).astype(F32)
        dg = dot_nt(R.go2[cc].reshape(128, 512), w_down()).astype(BF).astype(F32)
        th = jnp.tanh(GELU_K * (u + GELU_C * u * u * u))
        R.g2[cc] = (0.5 * u * (1.0 + th)).astype(BF)
        slope = 0.5 * (1.0 + th) + 0.5 * u * (1.0 - th * th) * (GELU_K * (1.0 + 3.0 * GELU_C * u * u))
        du = (dg * slope).astype(BF)
        R.du2[cc] = du
        return dot_nt(du, w_up())

    R.dao[...] = perceptron(c)
    got(K.a3, R.a32.at[0])
    R.das[...] = perceptron(1 - c).astype(BF)
    sib_push(K.da, R.das, R.dar)
    R.ops[...] = dot(R.g2[1 - c], w_down()).astype(BF)
    sib_push(K.op, R.ops, R.opr)
    R.oo[...] = dot(R.g2[c], w_down())

    def pack_rows(read, lo, hi, dst):
        def step(n, carry):
            base = 64 * (n // 2) + 8 * (n % 2)
            parts = [read[pl.ds(pl.multiple_of(base + 16 * k, 8), 8), lo:hi] for k in range(4)]
            dst[n] = jnp.concatenate(parts, 0).astype(BF)
            return carry

        lax.fori_loop(0, 16, step, 0)

    R.gus[...] = dot_tn(R.a32[...].reshape(256, 512), R.du2[...].reshape(256, 1024)).astype(BF).reshape(8, 4, 16, 1024)
    x_push(K.ux, lambda xx: R.gus.at[:, xx], R.gur)
    R.gur[x] = R.gus[:, x]
    for i in range(8):
        grad = dot_tn(R.g2[:, :, 128 * i : 128 * i + 128].reshape(256, 128), R.go2[...].reshape(256, 512)).astype(BF)
        for k in range(4):
            R.e1s[2 * i + k % 2, :, 512 * (k // 2) : 512 * (k // 2) + 512] = grad[32 * k : 32 * k + 32]

    plane_push(K.e1, R.e1s, R.e1r)
    R.e1r[i_me] = R.e1s[i_me]

    def sum4(ref):
        return (ref[0].astype(F32) + ref[1].astype(F32)) + (ref[2].astype(F32) + ref[3].astype(F32))

    def put_vector(at, row):
        for i in range(4):
            R.tb[at + i : at + i + 1, :] = row[:, 128 * i : 128 * i + 128]

    def put_halves(own, other, at, grad):
        width = grad.shape[1] // 2
        left, right = grad[:, 0:width], grad[:, width : 2 * width]
        own[:, at : at + width] = jnp.where(c == 0, left, right)
        other[:, at : at + width] = jnp.where(c == 0, right, left).astype(BF)

    got(K.da, R.dar)
    dthird = R.dao[...] + R.dar[...].astype(F32)
    n3 = R.n3[...]
    put_vector(16, column_sum(dthird * n3))
    put_vector(20, column_sum(dthird))
    dy = R.go2[c].reshape(128, 512).astype(F32)
    dx2 = dy + norm_back(dthird * R.gv[2:3, :], n3, R.i3[:, 0:1])
    R.dx2[...] = dx2
    dx2_low = dx2.astype(BF)
    do2 = dot_nt(dx2_low, c_out()).astype(BF)
    for i in range(4):
        R.do2[i] = do2[:, 128 * i : 128 * i + 128]

    def cross_back(i, carry):
        keys, values = cross_pair(i)
        R.dqc[i], dk, dv = attend_back(R.qc[i], R.do2[i], transposed(keys), values, R.p2[i])
        R.dkvc[:, :, :, pl.ds(pl.multiple_of(128 * i, 128), 128)] = dk.astype(BF).reshape(2, 4, 160, 128)
        R.dkvc[:, :, :, pl.ds(pl.multiple_of(512 + 128 * i, 128), 128)] = dv.astype(BF).reshape(2, 4, 160, 128)
        return carry

    lax.fori_loop(0, 4, cross_back, 0)
    sib_push(K.dkc, R.dkvc.at[1 - c], R.dkcr)

    dqc = own_columns(R.dqc)
    dsecond = dot_nt(dqc, c_query())
    n2 = R.n2[...]
    put_vector(8, column_sum(dsecond * n2))
    put_vector(12, column_sum(dsecond))
    dx1 = R.dx2[...] + norm_back(dsecond * R.gv[0:1, :], n2, R.i2[:, 0:1])
    R.dx1[...] = dx1
    dx1_low = dx1.astype(BF)
    do1 = dot_nt(dx1_low, w_out()).astype(BF)
    for i in range(4):
        R.do1s[i] = do1[:, 128 * i : 128 * i + 128]
    for d in (2, 1, 3):
        xx = (x + d) % 4
        push(K.do1, R.do1s.at[xx], R.do1r.at[x], did(b, xx, t, c), slot=do1_base + x)
    later(K.do1, R.do1r.at[0:3])
    R.do1r[x] = R.do1s[x]

    got(K.op, R.opr)
    R.outs[...] = (R.x2[...] + R.oo[...] + R.opr[...].astype(F32)).astype(BF).reshape(2, 64, 512)
    push(K.out, R.outs.at[1 - t], R.out_tok.at[t], partner)
    later(K.out, R.outs.at[0])
    R.out_tok[t] = R.outs[t]

    got(K.dkc, R.dkcr)

    def patch_back(i, carry):
        dkv = (R.dkvc[c, i].astype(F32) + R.dkcr[i].astype(F32)).astype(BF)
        R.dks[i] = dkv
        dpp = dot_nt(dkv, c_pair()).astype(BF)
        R.dpp[i] = dpp
        R.gps[i] = dot_nt(dpp, R.wp[...]).astype(BF)

        @pl.when(i != x)
        def _():
            push(K.gp, R.gps.at[i], R.gpr.at[x], did(b, i, t, c))

        return carry

    lax.fori_loop(0, 4, patch_back, 0)
    later(K.gp, R.gpr.at[0:3])
    R.gpr[x] = R.gps[x]
    grad = dot_tn(R.pp[...].reshape(640, 512), R.dks[...].reshape(640, 1024))
    put_halves(R.ga, R.gas, 0, grad[:, 0:512])
    put_halves(R.ga, R.gas, 256, grad[:, 512:1024])
    spread = dot(R.path[...].reshape(640, 384), spread_rows()).astype(BF)
    put_halves(R.ga, R.gas, 512, dot_tn(spread, R.dpp[...].reshape(640, 512)))
    put_halves(R.ga, R.gas, 768, dot_tn(own_columns(R.o2), R.dx2[...].astype(BF)))
    sib_push(K.ga, R.gas, R.gar)
    put_halves(R.gb2, R.gbs, 0, dot_tn(R.a2[...], dqc))
    put_halves(R.gb2, R.gbs, 256, dot_tn(own_columns(R.o1r), dx1_low))
    sib_push(K.gb, R.gbs, R.gbr)
    got(K.ga, R.gar)
    R.ga[...] += R.gar[...].astype(F32)
    R.kxs[...] = R.ga[:, 0:512].astype(BF).reshape(8, 4, 16, 512)
    x_push(K.kx, lambda xx: R.kxs.at[:, xx], R.kxr)
    R.kxr[x] = R.kxs[:, x]
    pack_rows(R.ga, 512, 1024, R.e2s)
    plane_push(K.e2, R.e2s, R.e2r)
    R.e2r[i_me] = R.e2s[i_me]
    got(K.gb, R.gbr)
    R.gb2[...] += R.gbr[...].astype(F32)
    pack_rows(R.gb2, 0, 512, R.e4s)
    plane_push(K.e4, R.e4s, R.e4r)
    R.e4r[i_me] = R.e4s[i_me]

    R.dkv[...] = jnp.zeros(R.dkv.shape, F32)

    def self_back(n, carry):
        xc = (x + 3 * n + (n // 2) * (7 - 2 * n)) % 4

        @pl.when(n > 0)
        def _():
            pltpu.make_async_copy(R.do1r.at[0], R.do1r.at[0], rs.at[do1_base + xc]).wait()

        R.dq[xc], dk, dv = attend_back(R.qs[xc], R.do1r[xc], R.kt[...], self_values(), R.p1[xc])
        R.dkv[:, :, 0:128] += dk.reshape(2, 512, 128)
        R.dkv[:, :, 128:256] += dv.reshape(2, 512, 128)
        return carry

    lax.fori_loop(0, 4, self_back, 0)
    R.dkvs[...] = R.dkv[1 - c].astype(BF)
    sib_push(K.dkv, R.dkvs, R.dkvr)
    R.dqkv[:, 0:128] = R.dq[...].reshape(512, 128)
    R.gc[:, 0:128] = dot_tn(R.a1h[...].reshape(512, 512), R.dqkv[:, 0:128])
    got(K.dkv, R.dkvr)
    R.dqkv[:, 128:384] = (R.dkv[c] + R.dkvr[...].astype(F32)).astype(BF)

    R.gc[:, 128:384] = dot_tn(R.a1h[...].reshape(512, 512), R.dqkv[:, 128:384])
    pack_rows(R.gc, 0, 384, R.e3s)
    plane_push(K.e3, R.e3s, R.e3r)
    R.e3r[i_me] = R.e3s[i_me]

    def first_step(i, sums):
        d1 = dot_nt(R.dqkv[pl.ds(pl.multiple_of(128 * i, 128), 128), :], R.wqkv[...].reshape(512, 384))
        R.d1s[i] = d1.astype(BF)

        @pl.when(i != x)
        def _():
            push(K.d1, R.d1s.at[i], R.d1r.at[x], did(b, i, t, c))

        return sums[0] + column_sum(d1 * R.n1h[i]), sums[1] + column_sum(d1)

    zero = jnp.zeros((1, 512), F32)
    dscale, dshift = lax.fori_loop(0, 4, first_step, (zero, zero))
    later(K.d1, R.d1r.at[0:3])
    R.d1r[x] = R.d1s[x]
    put_vector(0, dscale)
    put_vector(4, dshift)
    sib_push(K.tbs, R.tb, R.tbs)
    got(K.tbs, R.tbs)
    R.tbx[...] = R.tb[...] + R.tbs[...]
    x_push(K.tbx, lambda xx: R.tbx, R.tbr)
    R.tbr[x] = R.tbx[...]

    x_got(K.ux, R.gur)
    x_got(K.kx, R.kxr)

    def fold_step(n, carry):
        for ref, at, wide in ((R.gur, 0, 256), (R.kxr, 256, 128)):
            total = (ref[0, n].astype(F32) + ref[1, n].astype(F32)) + (ref[2, n].astype(F32) + ref[3, n].astype(F32))
            for k in range(2):
                parts = [total[8 * k : 8 * k + 8, wide * i : wide * i + wide] for i in range(4)]
                R.e5s[2 * n + k, :, at : at + wide] = jnp.concatenate(parts, 0).astype(BF)
        return carry

    lax.fori_loop(0, 8, fold_step, 0)
    plane_push(K.e5, R.e5s, R.e5r)
    R.e5r[i_me] = R.e5s[i_me]

    def rows_of(ref):
        return lambda xx: ref.at[pl.ds(pl.multiple_of(8 * xx, 8), 8)]

    def to_owners(name, src, dst):
        x_push(name, rows_of(src), dst)
        dst[x] = src[pl.ds(pl.multiple_of(8 * x, 8), 8), :]

    got(K.e1, R.e1r.at[0:15])
    total = plane_sum(R.e1r)
    R.dns[0] = total[:, 0:512]
    R.dns[1] = total[:, 512:1024]
    for k in range(2):
        owner = 2 * c + k

        @pl.when(x != owner)
        def _():
            push((K.dn0, K.dn1)[k], R.dns.at[k], R.dnr.at[x], did(b, owner, t, c), slot=K.dnr)

        later((K.dn0, K.dn1)[k], R.dns.at[k], x != owner)

        @pl.when(x == owner)
        def _():
            R.dnr[x] = R.dns[k]

    x_got(K.tbx, R.tbr)
    R.tbo[...] = (R.tbr[0] + R.tbr[1]) + (R.tbr[2] + R.tbr[3])
    plane_push(K.tbp, R.tbo, R.tbp)
    R.tbp[i_me] = R.tbo[...]

    x_got(K.d1, R.d1r)
    dfirst = sum4(R.d1r)
    n1, i1 = normalize(R.tokh[pl.ds(2 * x, 2)].reshape(128, 512).astype(F32))
    dstream = R.dx1[...] + norm_back(dfirst * scale_up, n1, i1)
    R.gts[...] = dstream.astype(BF).reshape(2, 64, 512)
    push(K.gt, R.gts.at[1 - t], R.g_tok.at[t], partner)
    later(K.gt, R.gts.at[0])
    R.g_tok[t] = R.gts[t]

    x_got(K.gp, R.gpr)
    R.gpo[...] = sum4(R.gpr).astype(BF).reshape(2, 80, 384)
    push(K.gpz, R.gpo.at[1 - t], R.g_pat.at[t], partner)
    later(K.gpz, R.gpo.at[0])
    R.g_pat[t] = R.gpo[t]

    got(K.e3, R.e3r.at[0:15])
    R.u3s[...] = plane_sum(R.e3r)
    to_owners(K.u3, R.u3s, R.u3r)

    got(K.e2, R.e2r.at[0:15])
    R.u2s[:, 0:512] = plane_sum(R.e2r)
    got(K.e4, R.e4r.at[0:15])
    R.u2s[:, 512:1024] = plane_sum(R.e4r)
    to_owners(K.u2, R.u2s, R.u2r)
    got(K.e5, R.e5r.at[0:15])
    total = plane_sum(R.e5r)
    for i in range(4):
        R.u1o[:, 256 * i : 256 * i + 256] = total[8 * i : 8 * i + 8, 0:256]
        R.u1o[:, 1024 + 128 * i : 1152 + 128 * i] = total[8 * i : 8 * i + 8, 256:384]
    sib_push(K.u1z, R.u1o, R.u1z)

    x_got(K.u3, R.u3r)
    sib_push(K.u3z, R.u3r, R.u3z)

    @pl.when(x // 2 == c)
    def _():
        x_got(K.dnr, R.dnr)
        R.dno[...] = (R.dnr[0] + R.dnr[1]) + (R.dnr[2] + R.dnr[3])
        push(K.dnz, R.dno.at[pl.ds(pl.multiple_of(16 - 16 * c, 16), 16)], R.dnz, sibling)

    later(K.dnz, R.dnz, x // 2 == c)
    x_got(K.u2, R.u2r)

    R.u2o[...] = (R.u2r[0] + R.u2r[1]) + (R.u2r[2] + R.u2r[3])
    sib_push(K.u2z, R.u2o, R.u2z)

    got(K.cam, R.camr.at[0:7])
    got(K.tbp, R.tbp.at[0:15])
    wanted = iota((8, 128), 1) == 8 * j + iota((8, 128), 0)
    acc = [jnp.zeros((8, 128), F32) for _ in range(8)]
    vec = jnp.zeros((16, 128), F32)
    for o in range(16):
        row = R.camr[o // 2, pl.ds(8 * (o % 2) + b, 1), :]
        weight = jnp.sum(jnp.where(wanted, row, 0.0), 1, keepdims=True)
        dmod = R.tbp[o, 0:8, :]
        for i in range(8):
            acc[i] = acc[i] + weight * dmod[i : i + 1, :]
        vec = vec + R.tbp[o, 8:24, :]
    for i in range(8):
        R.g_mod[:, 128 * i : 128 * i + 128] = acc[i]
    for v in range(4):
        for i in range(4):
            R.g_vec[v : v + 1, 128 * i : 128 * i + 128] = vec[4 * v + i : 4 * v + i + 1, :]

    def mine(v):
        return jnp.where(c == 0, v[0:4], v[4:8])

    def halves(own, other):
        return jnp.where(c == 0, own, other), jnp.where(c == 0, other, own)

    got(K.u3z, R.u3z)
    for k in range(4):
        total = mine(R.u3r[k] + R.u3z[k])
        for n, ref in enumerate((R.g_query, R.g_key, R.g_value)):
            ref[:, 128 * k : 128 * k + 128] = total[:, 128 * n : 128 * n + 128]
    got(K.u1z, R.u1z)
    for n, part in enumerate(halves(mine(R.u1o[...]), mine(R.u1z[...]))):
        for i in range(8):
            R.g_up[:, 256 * i + 128 * n : 256 * i + 128 * n + 128] = part[:, 128 * i : 128 * i + 128]
        R.g_ckey[:, 256 * n : 256 * n + 256] = part[:, 1024:1280]
        R.g_cvalue[:, 256 * n : 256 * n + 256] = part[:, 1280:1536]

    @pl.when(x // 2 == c)
    def _():
        R.g_down[...] = R.dno[pl.ds(pl.multiple_of(16 * c, 16), 16), :]

    @pl.when(x // 2 != c)
    def _():
        got(K.dnz, R.dnz)
        R.g_down[...] = R.dnz[...]

    got(K.u2z, R.u2z)
    for n, part in enumerate(halves(mine(R.u2o[...]), mine(R.u2z[...]))):
        for k, ref in enumerate((R.g_patch, R.g_cout, R.g_cquery, R.g_out)):
            rows = ref.shape[0]
            ref[:, 256 * n : 256 * n + 256] = part[0:rows, 256 * k : 256 * k + 256]

    got(K.out, R.outs.at[0])
    got(K.gt, R.gts.at[0])
    got(K.gpz, R.gpo.at[0])
    for name, like, when in pending:
        if when is None:
            sent(name, like)
        else:
            pl.when(when)(functools.partial(sent, name, like))


def copies(*refs):
    count = len(OUTPUTS) - 1
    sources, vectors, targets, parts = refs[:count], refs[count], refs[count + 1 : 2 * count + 1], refs[2 * count + 1 :]
    for source, target in zip(sources, targets):
        target[...] = source[...]
    at = 64 * lax.axis_index("batch") + 4 * lax.axis_index("blk")
    wanted = iota((4, 512), 1) == at + iota((4, 512), 0)
    for v, part in enumerate(parts):
        part[...] = jnp.sum(jnp.where(wanted, vectors[v : v + 1, :], 0.0), 1)


def hand_over(arrays):
    spec = pl.BlockSpec(memory_space=pltpu.VMEM)
    shapes = [jax.ShapeDtypeStruct(s, d) for s, d in OUTPUTS.values()][:-1]
    shapes += [jax.ShapeDtypeStruct((4,), F32)] * 4
    return pl.pallas_call(
        copies,
        out_shape=shapes,
        in_specs=[spec] * len(OUTPUTS),
        out_specs=[spec] * len(shapes),
        name="results",
    )(*arrays)


def on_device(
    tokens, patches, camera, counts, grad_out, w_mod, w_query, w_key, w_value, w_out, w_patch,
    c_query, c_key, c_value, c_out, gain_two, bias_two, gain_three, bias_three, w_up, w_down,
):
    vmem = pl.BlockSpec(memory_space=pltpu.VMEM)
    outs = pl.pallas_call(
        kernel,
        out_shape=[jax.ShapeDtypeStruct(s, d) for s, d in OUTPUTS.values()],
        in_specs=[pl.BlockSpec(memory_space=space) for space in INPUTS.values()],
        out_specs=[vmem] * len(OUTPUTS),
        scratch_shapes=[pltpu.VMEM(s, d) for s, d in SCRATCH.values()]
        + [pltpu.SemaphoreType.DMA((len(K),)), pltpu.SemaphoreType.DMA((len(K) + 4,))],
        compiler_params=pltpu.CompilerParams(
            collective_id=0, has_side_effects=True, vmem_limit_bytes=58 << 20
        ),
        name="layer",
    )(
        tokens, patches, camera, counts, grad_out, w_mod, w_query, w_key, w_value, w_out,
        w_patch, c_query, c_key, c_value, c_out, gain_two, bias_two, gain_three, bias_three, w_up, w_down,
    )
    *outs, g_gain_two, g_bias_two, g_gain_three, g_bias_three = hand_over(outs)
    return (*outs[:13], g_gain_two, g_bias_two, g_gain_three, g_bias_three, *outs[13:])


def solution(mesh):
    weight = P("blk", None)
    whole = P(("batch", "blk"), None)
    vector = P(("batch", "blk"))
    rows = P("batch", "blk", None)
    return jax.shard_map(
        on_device,
        mesh=mesh,
        in_specs=(
            rows, rows, P("batch", None), P("batch"), rows,
            *(weight,) * 10, *(P("blk"),) * 4, weight, weight,
        ),
        out_specs=(rows, rows, rows, *(whole,) * 10, *(vector,) * 4, whole, whole),
        check_vma=False,
    )
```

```python
import enum
import functools
import types

import jax
import jax.numpy as jnp
from jax import lax
from jax.experimental import pallas as pl
from jax.experimental.pallas import tpu as pltpu
from jax.sharding import PartitionSpec as P

F32 = jnp.float32
BF = jnp.bfloat16
MESH = pl.DeviceIdType.MESH
EPSILON = 1e-05
BIG_NEG = -1e30
GELU_K = 0.7978845608028654
GELU_C = 0.044715


def dot(left, right):
    return jnp.dot(left, right, preferred_element_type=F32)


def dot_nt(left, right):
    return lax.dot_general(left, right, (((1,), (1,)), ((), ())), preferred_element_type=F32)


def dot_tn(left, right):
    return lax.dot_general(left, right, (((0,), (0,)), ((), ())), preferred_element_type=F32)


def normalize(stream):
    centred = stream - jnp.mean(stream, -1, keepdims=True)
    inverse = lax.rsqrt(jnp.mean(centred * centred, -1, keepdims=True) + EPSILON)
    return centred * inverse, inverse


def norm_back(dnormed, normed, inverse):
    return inverse * (
        dnormed
        - jnp.mean(dnormed, -1, keepdims=True)
        - normed * jnp.mean(dnormed * normed, -1, keepdims=True)
    )


def column_sum(rows):
    return jnp.sum(rows, 0, keepdims=True)


def iota(shape, dim):
    return lax.broadcasted_iota(jnp.int32, shape, dim)


class Inputs:
    tok = pltpu.VMEM
    pat = pltpu.VMEM
    camera = pltpu.VMEM
    counts = pltpu.SMEM
    go = pltpu.VMEM
    w_mod = pltpu.VMEM
    w_query = pltpu.VMEM
    w_key = pltpu.VMEM
    w_value = pltpu.VMEM
    w_out = pltpu.VMEM
    w_patch = pltpu.VMEM
    c_query = pltpu.VMEM
    c_key = pltpu.VMEM
    c_value = pltpu.VMEM
    c_out = pltpu.VMEM
    gain_two = pltpu.VMEM
    bias_two = pltpu.VMEM
    gain_three = pltpu.VMEM
    bias_three = pltpu.VMEM
    w_up = pltpu.VMEM
    w_down = pltpu.VMEM


class Outputs:
    out_tok = ((2, 64, 512), BF)
    g_tok = ((2, 64, 512), BF)
    g_pat = ((2, 80, 384), BF)
    g_mod = ((8, 1024), F32)
    g_query = ((4, 512), F32)
    g_key = ((4, 512), F32)
    g_value = ((4, 512), F32)
    g_out = ((4, 512), F32)
    g_patch = ((3, 512), F32)
    g_cquery = ((4, 512), F32)
    g_ckey = ((4, 512), F32)
    g_cvalue = ((4, 512), F32)
    g_cout = ((4, 512), F32)
    g_up = ((4, 2048), F32)
    g_down = ((16, 512), F32)
    g_vec = ((4, 512), F32)


class Scratch:
    cam = ((16, 128), F32)
    tokh = ((8, 64, 512), BF)
    path = ((8, 80, 384), BF)
    wqs = ((4, 32, 384), BF)
    wfs = ((32, 1152), BF)
    wqkv = ((8, 2, 32, 384), BF)
    wf = ((8, 2, 32, 1152), BF)
    mods = ((2, 8, 128), F32)
    modr = ((8, 8, 128), F32)
    modo = ((8, 128), F32)
    modx = ((8, 128), F32)
    camr = ((8, 16, 128), F32)
    gv = ((8, 512), F32)
    bias = ((1280, 128), F32)
    n1h = ((4, 128, 512), F32)
    a1h = ((4, 128, 512), BF)
    qs = ((4, 128, 128), BF)
    kv = ((2, 4, 128, 256), BF)
    p1 = ((4, 1024, 256), BF)
    o1s = ((4, 128, 128), BF)
    o1r = ((4, 128, 128), BF)
    x1 = ((128, 512), F32)
    n2 = ((128, 512), F32)
    i2 = ((128, 128), F32)
    a2 = ((128, 512), BF)
    wk = ((8, 2, 32, 1536), BF)
    kvc = ((2, 4, 160, 1024), BF)
    p2 = ((4, 1280, 256), BF)
    x2 = ((128, 512), F32)
    n3 = ((128, 512), F32)
    i3 = ((128, 128), F32)
    das = ((128, 512), BF)
    dar = ((128, 512), BF)
    ops = ((128, 512), BF)
    opr = ((128, 512), BF)
    outs = ((2, 64, 512), BF)
    dx2 = ((128, 512), F32)
    dkvc = ((2, 4, 160, 1024), BF)
    dkcr = ((4, 160, 1024), BF)
    gps = ((4, 160, 384), BF)
    gpr = ((4, 160, 384), BF)
    gpo = ((2, 80, 384), BF)
    dx1 = ((128, 512), F32)
    do1s = ((4, 128, 128), BF)
    do1r = ((4, 128, 128), BF)
    dkv = ((2, 512, 256), F32)
    dkvs = ((512, 256), BF)
    dkvr = ((512, 256), BF)
    dqkv = ((512, 384), BF)
    d1s = ((4, 128, 512), BF)
    d1r = ((4, 128, 512), BF)
    gts = ((2, 64, 512), BF)
    dq = ((4, 128, 128), BF)
    gb2 = ((512, 512), F32)
    gbs = ((512, 512), BF)
    gbr = ((512, 512), BF)
    gc = ((512, 384), F32)
    e1s = ((16, 32, 1024), BF)
    e1r = ((16, 32, 1024), BF)
    e2s = ((16, 32, 512), BF)
    e2r = ((16, 32, 512), BF)
    e3s = ((16, 32, 384), BF)
    e3r = ((16, 32, 384), BF)
    u1o = ((8, 1536), F32)
    u1z = ((8, 1536), F32)
    dns = ((2, 32, 512), F32)
    dnr = ((4, 32, 512), F32)
    dnz = ((16, 512), F32)
    u2s = ((32, 1024), F32)
    u2r = ((4, 8, 1024), F32)
    u2o = ((8, 1024), F32)
    u2z = ((8, 1024), F32)
    u3s = ((32, 384), F32)
    u3r = ((4, 8, 384), F32)
    u3z = ((4, 8, 384), F32)
    tb = ((24, 128), F32)
    tbs = ((24, 128), F32)
    tbx = ((24, 128), F32)
    tbr = ((4, 24, 128), F32)
    tbo = ((24, 128), F32)
    tbp = ((16, 24, 128), F32)
    wks = ((32, 1536), BF)
    kt = ((128, 1024), BF)
    vt = ((128, 1024), BF)
    wp = ((384, 512), BF)
    pp = ((4, 160, 512), BF)
    qc = ((4, 128, 128), BF)
    o2 = ((4, 128, 128), BF)
    do2 = ((4, 128, 128), BF)
    dqc = ((4, 128, 128), BF)
    dks = ((4, 160, 1024), BF)
    dpp = ((4, 160, 512), BF)
    w3s = ((32, 1024), BF)
    w3m = ((2, 32, 1024), BF)
    w3 = ((8, 2, 32, 1024), BF)
    w4 = ((8, 128, 512), BF)
    go2 = ((2, 2, 64, 512), BF)
    a32 = ((2, 128, 512), BF)
    g2 = ((2, 128, 1024), BF)
    du2 = ((2, 128, 1024), BF)
    dao = ((128, 512), F32)
    oo = ((128, 512), F32)
    dno = ((32, 512), F32)
    gus = ((8, 4, 16, 1024), BF)
    gur = ((4, 8, 16, 1024), BF)
    ga = ((512, 1024), F32)
    gas = ((512, 1024), BF)
    gar = ((512, 1024), BF)
    e4s = ((16, 32, 512), BF)
    e4r = ((16, 32, 512), BF)
    co = ((8, 2, 32, 512), BF)
    kxs = ((8, 4, 16, 512), BF)
    kxr = ((4, 8, 16, 512), BF)
    e5s = ((16, 32, 384), BF)
    e5r = ((16, 32, 384), BF)


def members(group):
    return {name: value for name, value in vars(group).items() if not name.startswith("_")}


INPUTS, OUTPUTS, SCRATCH = members(Inputs), members(Outputs), members(Scratch)


class K(enum.IntEnum):
    a3 = 0
    cam = 1
    d1 = 2
    da = 3
    dkc = 4
    dkv = 5
    dn0 = 6
    dn1 = 7
    dnr = 8
    dnz = 9
    do1 = 10
    e1 = 11
    e2 = 12
    e3 = 13
    e4 = 14
    e5 = 15
    ga = 16
    gb = 17
    go = 18
    gox = 19
    gp = 20
    gpz = 21
    gt = 22
    kv = 23
    kvc = 24
    kx = 25
    mod = 26
    modx = 27
    o1 = 28
    op = 29
    out = 30
    pat = 31
    tbp = 32
    tbs = 33
    tbx = 34
    tok = 35
    u1z = 36
    u2 = 37
    u2z = 38
    u3 = 39
    u3z = 40
    ux = 41
    w1a = 42
    w1b = 43
    w1c = 44
    w1d = 45
    w2a = 46
    w2b = 47
    w2c = 48
    w2d = 49
    w3 = 50
    w3x = 51
    w4a = 52
    w4b = 53
    w4c = 54
    w5 = 55
    w5d = 56
    wq = 57
    wqx = 58


def kernel(*refs):
    *buffers, ss, rs = refs
    R = types.SimpleNamespace(**dict(zip((*INPUTS, *OUTPUTS, *SCRATCH), buffers)))
    b = lax.axis_index("batch")
    j = lax.axis_index("blk")
    x = j // 4
    t = (j // 2) % 2
    c = j % 2
    p = 2 * x + t
    i_me = 2 * b + t

    def did(bb, xx, tt, cc):
        return (bb, xx * 4 + tt * 2 + cc)

    pending = []
    do1_base = len(K)

    def push(name, src, dst, dev, slot=None):
        pltpu.make_async_remote_copy(
            src_ref=src,
            dst_ref=dst,
            send_sem=ss.at[name],
            recv_sem=rs.at[name if slot is None else slot],
            device_id=dev,
            device_id_type=MESH,
        ).start()

    def got(name, like):
        pltpu.make_async_copy(like, like, rs.at[name]).wait()

    def sent(name, like):
        pltpu.make_async_copy(like, like, ss.at[name]).wait()

    def later(name, like, when=None):
        pending.append((name, like, when))

    sibling = did(b, x, t, 1 - c)
    partner = did(b, x, 1 - t, c)
    near = [((x + dx) % 4, (t + dt) % 2) for dx, dt in ((0, 1), (1, 0), (3, 0), (2, 0), (1, 1), (3, 1), (2, 1))]

    def near_push(name, src_of, dst, like):
        for xx, tt in near:
            push(name, src_of(xx, tt), dst, did(b, xx, tt, c))
        later(name, like)

    def x_push(name, src_of, dst_ref):
        for d in (1, 3, 2):
            xx = (x + d) % 4
            push(name, src_of(xx), dst_ref.at[x], did(b, xx, t, c))
        later(name, dst_ref.at[0:3])

    def x_got(name, dst_ref):
        got(name, dst_ref.at[0:3])

    def sib_push(name, src, dst):
        push(name, src, dst, sibling)
        later(name, dst)

    def plane_push(name, src, dst):
        def step(n, carry):
            bb = (b + n // 2) % 8
            tt = (t + n % 2) % 2
            pltpu.make_async_remote_copy(
                src_ref=src.at[2 * bb + tt] if src.shape[0] == 16 else src,
                dst_ref=dst.at[i_me],
                send_sem=ss.at[name],
                recv_sem=rs.at[name],
                device_id=did(bb, x, tt, c),
                device_id_type=MESH,
            ).start()
            return carry

        lax.fori_loop(1, 16, step, 0)
        later(name, dst.at[0:15])

    def plane_sum(ref):
        def step(n, acc):
            return acc + ref[n].astype(F32)

        return lax.fori_loop(1, 16, step, ref[0].astype(F32))

    for i in range(4):
        cols = slice(128 * i, 128 * i + 128)
        R.wqs[i, :, 0:128] = R.w_query[:, cols]
        R.wqs[i, :, 128:256] = R.w_key[:, cols]
        R.wqs[i, :, 256:384] = R.w_value[:, cols]
    lanes = iota((1, 128), 1)
    half = jnp.where(lanes // 64 == c, 1.0, 0.0).astype(F32)
    for o in range(2):
        for i in range(8):
            R.cam[8 * o + i : 8 * o + i + 1, :] = R.camera[o : o + 1, 128 * i : 128 * i + 128].astype(F32)
    row0 = R.cam[pl.ds(j // 2, 1), :] * half
    row1 = R.cam[pl.ds(8 + j // 2, 1), :] * half
    rows = jnp.concatenate([row0, row1, jnp.zeros((14, 128), F32)], 0).astype(BF)
    w_mod = R.w_mod[...]
    modp = dot(rows, jnp.concatenate([w_mod, w_mod], 0))
    for i in range(8):
        R.mods[0, i : i + 1, :] = modp[0:1, 128 * i : 128 * i + 128]
        R.mods[1, i : i + 1, :] = modp[1:2, 128 * i : 128 * i + 128]

    bar = pltpu.get_barrier_semaphore()

    def greet(dev):
        pl.semaphore_signal(bar, inc=1, device_id=dev, device_id_type=MESH)

    for xx, tt in near:
        greet(did(b, xx, tt, c))
    greet(sibling)

    def greet_plane(n, carry):
        greet(did((b + n // 2) % 8, x, (t + n % 2) % 2, c))
        return carry

    lax.fori_loop(1, 16, greet_plane, 0)

    pl.semaphore_wait(bar, 7 + 1 + 15)

    near_push(K.mod, lambda xx, tt: R.mods.at[tt], R.modr.at[p], R.modr.at[0:7])
    near_push(K.tok, lambda xx, tt: R.tok.at[tt], R.tokh.at[p], R.tokh.at[0:7])
    near_push(K.wq, lambda xx, tt: R.wqs.at[xx], R.wqkv.at[p, c], R.wqkv.at[0:7, 0])

    y = b % 4
    xs = (x + y) % 4
    xd = (x + 4 - y) % 4

    def spread_first(same, cross, src, whole):
        push(cross, src, slot(whole, p), did(b, xd, 1 - t, c))
        later(cross, src)

        @pl.when(y > 0)
        def _():
            push(same, src, slot(whole, p), did(b, xd, t, c))

        later(same, src, y > 0)

        @pl.when(y == 0)
        def _():
            slot(whole, p)[...] = src[...]

    def spread_second(same, cross, name, whole):
        got(cross, slot(whole, 0))

        @pl.when(y > 0)
        def _():
            got(same, slot(whole, 0))

        held = slot(whole, pl.ds(2 * xs, 2))
        for d in (2, 1, 3):
            push(name, held, held, did(b - y + (y + d) % 4, x, t, c))
        later(name, slot(whole, slice(0, 6)))

    def slot(whole, at):
        return whole.at[at, c] if len(whole.shape) == 4 else whole.at[at]

    def spread_third(name, whole):
        got(name, slot(whole, slice(0, 6)))

    def spread_last(name, whole):
        sib_push(name, whole.at[:, c], whole.at[:, c])

    f = iota((32, 24), 1)
    apart = jnp.where(iota((32, 24), 0) == f + (f * 21846) // 65536, 1.0, 0.0).astype(BF)
    R.wks[:, 0:512] = R.c_key[...]
    R.wks[:, 512:1024] = R.c_value[...]
    R.wks[:, 1024:1536] = dot(apart, R.w_patch[...]).astype(BF)
    R.wfs[:, 0:512] = R.w_out[...]
    R.wfs[:, 512:1024] = R.c_query[...]
    row = jnp.zeros((1, 128), F32)
    for v, ref in enumerate((R.gain_two, R.bias_two, R.gain_three, R.bias_three)):
        place = jnp.where(iota((32, 128), 1) == 32 * v + iota((32, 128), 0), 1.0, 0.0).astype(BF)
        row = row + dot(ref[...].reshape(1, 32), place)
    R.wfs[:, 1024:1152] = jnp.broadcast_to(row, (32, 128)).astype(BF)
    for i in range(8):
        left, right = R.w_up[:, 256 * i : 256 * i + 128], R.w_up[:, 256 * i + 128 : 256 * i + 256]
        R.w3s[:, 128 * i : 128 * i + 128] = jnp.where(c == 0, right, left)
        R.w3m[c, :, 128 * i : 128 * i + 128] = jnp.where(c == 0, left, right)
    sib_push(K.w3x, R.w3s, R.w3m.at[c])

    R.modr[p] = R.mods[t]
    R.co[p, c] = R.c_out[...]
    R.tokh[p] = R.tok[t]
    R.wqkv[p, c] = R.wqs[x]
    R.path[p] = R.pat[t]
    R.go2[c, t] = R.go[t]
    R.camr[b] = R.cam[...]

    got(K.mod, R.modr.at[0:7])
    spread_first(K.w1a, K.w1b, R.wks, R.wk)
    spread_first(K.w2a, K.w2b, R.wfs, R.wf)
    spread_first(K.w4a, K.w4b, R.w_down, R.w4)
    R.modo[...] = jnp.sum(R.modr[...], 0)
    sib_push(K.modx, R.modo, R.modx)

    got(K.wq, R.wqkv.at[0:7, 0])
    sib_push(K.wqx, R.wqkv.at[:, c], R.wqkv.at[:, c])

    got(K.tok, R.tokh.at[0:7])

    def norm_step(i, carry):
        R.n1h[i] = normalize(R.tokh[pl.ds(2 * i, 2)].reshape(128, 512).astype(F32))[0]
        return carry

    lax.fori_loop(0, 4, norm_step, 0)

    got(K.modx, R.modx)
    modv = R.modo[...] + R.modx[...]
    scale_up = 1.0 + jnp.concatenate([modv[i : i + 1, :] for i in range(4)], 1)
    shift = jnp.concatenate([modv[i : i + 1, :] for i in range(4, 8)], 1)
    got(K.wqx, R.wqkv.at[:, 0])

    def qkv_step(i, carry):
        a1 = (R.n1h[i] * scale_up + shift).astype(BF)
        R.a1h[i] = a1
        qkv = dot(a1, R.wqkv[...].reshape(512, 384))
        R.qs[i] = (qkv[:, 0:128].astype(BF).astype(F32) * 0.125).astype(BF)
        R.kv[c, i] = qkv[:, 128:384].astype(BF)
        return carry

    spread_second(K.w1a, K.w1b, K.w1c, R.wk)
    lax.fori_loop(0, 4, qkv_step, 0)
    sib_push(K.kv, R.kv.at[c], R.kv.at[c])
    spread_second(K.w2a, K.w2b, K.w2c, R.wf)
    near_push(K.pat, lambda xx, tt: R.pat.at[tt], R.path.at[p], R.path.at[0:7])
    near_push(K.w5, lambda xx, tt: R.c_out, R.co.at[p, c], R.co.at[0:7, 0])
    push(K.go, R.go.at[1 - t], R.go2.at[c, t], partner)
    later(K.go, R.go.at[0])

    def cam_step(n, carry):
        pltpu.make_async_remote_copy(
            src_ref=R.cam,
            dst_ref=R.camr.at[b],
            send_sem=ss.at[K.cam],
            recv_sem=rs.at[K.cam],
            device_id=did((b + n) % 8, x, t, c),
            device_id_type=MESH,
        ).start()
        return carry
    lax.fori_loop(1, 8, cam_step, 0)
    later(K.cam, R.camr.at[0:7])

    eye = jnp.where(iota((128, 128), 0) == iota((128, 128), 1), 1.0, 0.0).astype(BF)
    mask0 = jnp.where(iota((1, 128), 1) < 64, 1.0, 0.0).astype(BF)
    mask1 = jnp.where(iota((1, 128), 1) < 64, 0.0, 1.0).astype(BF)

    def transposed(rows):
        return dot_nt(eye, rows).astype(BF)

    def two_heads(rows):
        return jnp.concatenate([rows * mask0, rows * mask1], 0)

    def unfold(columns):
        return jnp.concatenate([columns[0:64, 0:128], columns[64:128, 128:256]], 0).T

    def attend(queries, keys, values_t, off):
        scores = dot_nt(keys, two_heads(queries))
        if off is not None:
            scores = scores + jnp.concatenate([off, off], 1)
        raised = jnp.exp(scores - jnp.max(scores, 0, keepdims=True))
        weights = (raised * (1.0 / jnp.sum(raised, 0, keepdims=True))).astype(BF)
        return weights, unfold(dot(values_t, weights)).astype(BF)

    def attend_back(queries, douts, keys_t, values, weights_low):
        q, dout = two_heads(queries), two_heads(douts)
        weights = weights_low.astype(F32)
        dweights = dot_nt(values, dout)
        delta = jnp.sum(weights * dweights, 0, keepdims=True)
        dscores = (weights * (dweights - delta)).astype(BF)
        dquery = (unfold(dot(keys_t, dscores)) * 0.125).astype(BF)
        return dquery, dot(dscores, q), dot(weights_low, dout)

    def own_columns(ref):
        return jnp.concatenate([ref[i] for i in range(4)], 1)

    got(K.kv, R.kv.at[0])

    def self_keys():
        return R.kv[:, :, :, 0:128].reshape(1024, 128)

    def self_values():
        return R.kv[:, :, :, 128:256].reshape(1024, 128)

    R.kt[...] = transposed(self_keys())
    R.vt[...] = transposed(self_values())

    def self_step(n, carry):
        xc = (x + 2 + 3 * n + (n // 2) * (7 - 2 * n)) % 4
        weights, out = attend(R.qs[xc], self_keys(), R.vt[...], None)
        R.p1[xc] = weights
        R.o1s[xc] = out

        @pl.when(n < 3)
        def _():
            push(K.o1, R.o1s.at[xc], R.o1r.at[x], did(b, xc, t, c))

        return carry

    lax.fori_loop(0, 4, self_step, 0)
    later(K.o1, R.o1r.at[0:3])
    R.o1r[x] = R.o1s[x]

    spread_third(K.w2c, R.wf)
    spread_last(K.w2d, R.wf)
    spread_second(K.w4a, K.w4b, K.w4c, R.w4)
    got(K.w3x, R.w3s)
    R.w3[p] = R.w3m[...]
    near_push(K.w3, lambda xx, tt: R.w3m, R.w3.at[p], R.w3.at[0:7])
    spread_third(K.w1c, R.wk)
    spread_last(K.w1d, R.wk)
    got(K.go, R.go2.at[0, 0])
    sib_push(K.gox, R.go2.at[c], R.go2.at[c])

    live = R.counts[t]
    for cc in range(2):
        for pp in range(8):
            slots = iota((80, 128), 0) + 80 * (2 * pp + cc)
            R.bias[640 * cc + 80 * pp : 640 * cc + 80 * pp + 80, :] = jnp.where(slots < live, 0.0, BIG_NEG)

    def w_out():
        return R.wf[:, :, :, 0:512].reshape(512, 512)

    def c_query():
        return R.wf[:, :, :, 512:1024].reshape(512, 512)

    def c_out():
        return R.co[...].reshape(512, 512)

    def c_pair():
        return R.wk[:, :, :, 0:1024].reshape(512, 1024)

    def spread_rows():
        f = iota((384, 512), 0)
        return jnp.where(iota((384, 512), 1) == f + (f * 21846) // 65536, 1.0, 0.0).astype(BF)

    got(K.w1d, R.wk.at[:, 0])
    R.wp[...] = dot(spread_rows(), R.wk[:, :, :, 1024:1536].reshape(512, 512)).astype(BF)
    got(K.pat, R.path.at[0:7])

    def patch_step(i, carry):
        projected = dot(R.path[pl.ds(2 * i, 2)].reshape(160, 384), R.wp[...]).astype(BF)
        R.pp[i] = projected
        R.kvc[c, i] = dot(projected, c_pair()).astype(BF)
        push(K.kvc, R.kvc.at[c, i], R.kvc.at[c, i], sibling)
        return carry

    lax.fori_loop(0, 4, patch_step, 0)
    later(K.kvc, R.kvc.at[0])

    got(K.w2d, R.wf.at[:, 0])
    packed = R.wf[:, :, :, 1024:1152].reshape(512, 128)
    pick = jnp.where(iota((16, 512), 1) == 32 * iota((16, 512), 0), 1.0, 0.0).astype(BF)
    vectors = dot(pick, packed).astype(BF)
    for v in range(4):
        spread = jnp.where(iota((128, 512), 0) == 32 * v + iota((128, 512), 1) % 32, 1.0, 0.0).astype(BF)
        placed = jnp.where(iota((16, 512), 1) // 32 == iota((16, 512), 0), dot(vectors, spread), 0.0)
        R.gv[v : v + 1, :] = column_sum(placed)

    x_got(K.o1, R.o1r)
    x1 = R.tokh[pl.ds(2 * x, 2)].reshape(128, 512).astype(F32) + dot(own_columns(R.o1r), w_out())
    R.x1[...] = x1
    n2, i2 = normalize(x1)
    R.n2[...] = n2
    R.i2[...] = jnp.broadcast_to(i2, (128, 128))
    a2 = (n2 * R.gv[0:1, :] + R.gv[1:2, :]).astype(BF)
    R.a2[...] = a2
    qc = (dot(a2, c_query()).astype(BF).astype(F32) * 0.125).astype(BF)
    for i in range(4):
        R.qc[i] = qc[:, 128 * i : 128 * i + 128]


    got(K.kvc, R.kvc.at[0])

    def cross_pair(i):
        keys = R.kvc[:, :, :, pl.ds(pl.multiple_of(128 * i, 128), 128)].reshape(1280, 128)
        values = R.kvc[:, :, :, pl.ds(pl.multiple_of(512 + 128 * i, 128), 128)].reshape(1280, 128)
        return keys, values

    def cross_step(i, carry):
        keys, values = cross_pair(i)
        R.p2[i], R.o2[i] = attend(R.qc[i], keys, transposed(values), R.bias[...])
        return carry

    lax.fori_loop(0, 4, cross_step, 0)
    got(K.w5, R.co.at[0:7, 0])
    spread_last(K.w5d, R.co)
    got(K.w5d, R.co.at[:, 0])
    x2 = R.x1[...] + dot(own_columns(R.o2), c_out())
    R.x2[...] = x2
    n3, i3 = normalize(x2)
    R.n3[...] = n3
    R.i3[...] = jnp.broadcast_to(i3, (128, 128))
    a3 = (n3 * R.gv[2:3, :] + R.gv[3:4, :]).astype(BF)
    R.a32[c] = a3
    sib_push(K.a3, R.a32.at[c], R.a32.at[c])

    got(K.w3, R.w3.at[0:7])
    spread_third(K.w4c, R.w4)
    got(K.gox, R.go2.at[0])

    def w_up():
        return R.w3[...].reshape(512, 1024)

    def w_down():
        return R.w4[...].reshape(1024, 512)

    def perceptron(cc):
        u = dot(R.a32[cc], w_up()).astype(BF).astype(F32)
        dg = dot_nt(R.go2[cc].reshape(128, 512), w_down()).astype(BF).astype(F32)
        th = jnp.tanh(GELU_K * (u + GELU_C * u * u * u))
        R.g2[cc] = (0.5 * u * (1.0 + th)).astype(BF)
        slope = 0.5 * (1.0 + th) + 0.5 * u * (1.0 - th * th) * (GELU_K * (1.0 + 3.0 * GELU_C * u * u))
        du = (dg * slope).astype(BF)
        R.du2[cc] = du
        return dot_nt(du, w_up())

    R.dao[...] = perceptron(c)
    got(K.a3, R.a32.at[0])
    R.das[...] = perceptron(1 - c).astype(BF)
    sib_push(K.da, R.das, R.dar)
    R.ops[...] = dot(R.g2[1 - c], w_down()).astype(BF)
    sib_push(K.op, R.ops, R.opr)
    R.oo[...] = dot(R.g2[c], w_down())

    def pack_rows(read, lo, hi, dst):
        def step(n, carry):
            base = 64 * (n // 2) + 8 * (n % 2)
            parts = [read[pl.ds(pl.multiple_of(base + 16 * k, 8), 8), lo:hi] for k in range(4)]
            dst[n] = jnp.concatenate(parts, 0).astype(BF)
            return carry

        lax.fori_loop(0, 16, step, 0)

    R.gus[...] = dot_tn(R.a32[...].reshape(256, 512), R.du2[...].reshape(256, 1024)).astype(BF).reshape(8, 4, 16, 1024)
    x_push(K.ux, lambda xx: R.gus.at[:, xx], R.gur)
    R.gur[x] = R.gus[:, x]
    for i in range(8):
        grad = dot_tn(R.g2[:, :, 128 * i : 128 * i + 128].reshape(256, 128), R.go2[...].reshape(256, 512)).astype(BF)
        for k in range(4):
            R.e1s[2 * i + k % 2, :, 512 * (k // 2) : 512 * (k // 2) + 512] = grad[32 * k : 32 * k + 32]

    plane_push(K.e1, R.e1s, R.e1r)
    R.e1r[i_me] = R.e1s[i_me]

    def sum4(ref):
        return (ref[0].astype(F32) + ref[1].astype(F32)) + (ref[2].astype(F32) + ref[3].astype(F32))

    def put_vector(at, row):
        for i in range(4):
            R.tb[at + i : at + i + 1, :] = row[:, 128 * i : 128 * i + 128]

    def put_halves(own, other, at, grad):
        width = grad.shape[1] // 2
        left, right = grad[:, 0:width], grad[:, width : 2 * width]
        own[:, at : at + width] = jnp.where(c == 0, left, right)
        other[:, at : at + width] = jnp.where(c == 0, right, left).astype(BF)

    got(K.da, R.dar)
    dthird = R.dao[...] + R.dar[...].astype(F32)
    n3 = R.n3[...]
    put_vector(16, column_sum(dthird * n3))
    put_vector(20, column_sum(dthird))
    dy = R.go2[c].reshape(128, 512).astype(F32)
    dx2 = dy + norm_back(dthird * R.gv[2:3, :], n3, R.i3[:, 0:1])
    R.dx2[...] = dx2
    dx2_low = dx2.astype(BF)
    do2 = dot_nt(dx2_low, c_out()).astype(BF)
    for i in range(4):
        R.do2[i] = do2[:, 128 * i : 128 * i + 128]

    def cross_back(i, carry):
        keys, values = cross_pair(i)
        R.dqc[i], dk, dv = attend_back(R.qc[i], R.do2[i], transposed(keys), values, R.p2[i])
        R.dkvc[:, :, :, pl.ds(pl.multiple_of(128 * i, 128), 128)] = dk.astype(BF).reshape(2, 4, 160, 128)
        R.dkvc[:, :, :, pl.ds(pl.multiple_of(512 + 128 * i, 128), 128)] = dv.astype(BF).reshape(2, 4, 160, 128)
        return carry

    lax.fori_loop(0, 4, cross_back, 0)
    sib_push(K.dkc, R.dkvc.at[1 - c], R.dkcr)

    dqc = own_columns(R.dqc)
    dsecond = dot_nt(dqc, c_query())
    n2 = R.n2[...]
    put_vector(8, column_sum(dsecond * n2))
    put_vector(12, column_sum(dsecond))
    dx1 = R.dx2[...] + norm_back(dsecond * R.gv[0:1, :], n2, R.i2[:, 0:1])
    R.dx1[...] = dx1
    dx1_low = dx1.astype(BF)
    do1 = dot_nt(dx1_low, w_out()).astype(BF)
    for i in range(4):
        R.do1s[i] = do1[:, 128 * i : 128 * i + 128]
    for d in (2, 1, 3):
        xx = (x + d) % 4
        push(K.do1, R.do1s.at[xx], R.do1r.at[x], did(b, xx, t, c), slot=do1_base + x)
    later(K.do1, R.do1r.at[0:3])
    R.do1r[x] = R.do1s[x]

    got(K.op, R.opr)
    R.outs[...] = (R.x2[...] + R.oo[...] + R.opr[...].astype(F32)).astype(BF).reshape(2, 64, 512)
    push(K.out, R.outs.at[1 - t], R.out_tok.at[t], partner)
    later(K.out, R.outs.at[0])
    R.out_tok[t] = R.outs[t]

    got(K.dkc, R.dkcr)

    def patch_back(i, carry):
        dkv = (R.dkvc[c, i].astype(F32) + R.dkcr[i].astype(F32)).astype(BF)
        R.dks[i] = dkv
        dpp = dot_nt(dkv, c_pair()).astype(BF)
        R.dpp[i] = dpp
        R.gps[i] = dot_nt(dpp, R.wp[...]).astype(BF)

        @pl.when(i != x)
        def _():
            push(K.gp, R.gps.at[i], R.gpr.at[x], did(b, i, t, c))

        return carry

    lax.fori_loop(0, 4, patch_back, 0)
    later(K.gp, R.gpr.at[0:3])
    R.gpr[x] = R.gps[x]
    grad = dot_tn(R.pp[...].reshape(640, 512), R.dks[...].reshape(640, 1024))
    put_halves(R.ga, R.gas, 0, grad[:, 0:512])
    put_halves(R.ga, R.gas, 256, grad[:, 512:1024])
    spread = dot(R.path[...].reshape(640, 384), spread_rows()).astype(BF)
    put_halves(R.ga, R.gas, 512, dot_tn(spread, R.dpp[...].reshape(640, 512)))
    put_halves(R.ga, R.gas, 768, dot_tn(own_columns(R.o2), R.dx2[...].astype(BF)))
    sib_push(K.ga, R.gas, R.gar)
    put_halves(R.gb2, R.gbs, 0, dot_tn(R.a2[...], dqc))
    put_halves(R.gb2, R.gbs, 256, dot_tn(own_columns(R.o1r), dx1_low))
    sib_push(K.gb, R.gbs, R.gbr)
    got(K.ga, R.gar)
    R.ga[...] += R.gar[...].astype(F32)
    R.kxs[...] = R.ga[:, 0:512].astype(BF).reshape(8, 4, 16, 512)
    x_push(K.kx, lambda xx: R.kxs.at[:, xx], R.kxr)
    R.kxr[x] = R.kxs[:, x]
    pack_rows(R.ga, 512, 1024, R.e2s)
    plane_push(K.e2, R.e2s, R.e2r)
    R.e2r[i_me] = R.e2s[i_me]
    got(K.gb, R.gbr)
    R.gb2[...] += R.gbr[...].astype(F32)
    pack_rows(R.gb2, 0, 512, R.e4s)
    plane_push(K.e4, R.e4s, R.e4r)
    R.e4r[i_me] = R.e4s[i_me]

    R.dkv[...] = jnp.zeros(R.dkv.shape, F32)

    def self_back(n, carry):
        xc = (x + 3 * n + (n // 2) * (7 - 2 * n)) % 4

        @pl.when(n > 0)
        def _():
            pltpu.make_async_copy(R.do1r.at[0], R.do1r.at[0], rs.at[do1_base + xc]).wait()

        R.dq[xc], dk, dv = attend_back(R.qs[xc], R.do1r[xc], R.kt[...], self_values(), R.p1[xc])
        R.dkv[:, :, 0:128] += dk.reshape(2, 512, 128)
        R.dkv[:, :, 128:256] += dv.reshape(2, 512, 128)
        return carry

    lax.fori_loop(0, 4, self_back, 0)
    R.dkvs[...] = R.dkv[1 - c].astype(BF)
    sib_push(K.dkv, R.dkvs, R.dkvr)
    R.dqkv[:, 0:128] = R.dq[...].reshape(512, 128)
    R.gc[:, 0:128] = dot_tn(R.a1h[...].reshape(512, 512), R.dqkv[:, 0:128])
    got(K.dkv, R.dkvr)
    R.dqkv[:, 128:384] = (R.dkv[c] + R.dkvr[...].astype(F32)).astype(BF)

    R.gc[:, 128:384] = dot_tn(R.a1h[...].reshape(512, 512), R.dqkv[:, 128:384])
    pack_rows(R.gc, 0, 384, R.e3s)
    plane_push(K.e3, R.e3s, R.e3r)
    R.e3r[i_me] = R.e3s[i_me]

    def first_step(i, sums):
        d1 = dot_nt(R.dqkv[pl.ds(pl.multiple_of(128 * i, 128), 128), :], R.wqkv[...].reshape(512, 384))
        R.d1s[i] = d1.astype(BF)

        @pl.when(i != x)
        def _():
            push(K.d1, R.d1s.at[i], R.d1r.at[x], did(b, i, t, c))

        return sums[0] + column_sum(d1 * R.n1h[i]), sums[1] + column_sum(d1)

    zero = jnp.zeros((1, 512), F32)
    dscale, dshift = lax.fori_loop(0, 4, first_step, (zero, zero))
    later(K.d1, R.d1r.at[0:3])
    R.d1r[x] = R.d1s[x]
    put_vector(0, dscale)
    put_vector(4, dshift)
    sib_push(K.tbs, R.tb, R.tbs)
    got(K.tbs, R.tbs)
    R.tbx[...] = R.tb[...] + R.tbs[...]
    x_push(K.tbx, lambda xx: R.tbx, R.tbr)
    R.tbr[x] = R.tbx[...]

    x_got(K.ux, R.gur)
    x_got(K.kx, R.kxr)

    def fold_step(n, carry):
        for ref, at, wide in ((R.gur, 0, 256), (R.kxr, 256, 128)):
            total = (ref[0, n].astype(F32) + ref[1, n].astype(F32)) + (ref[2, n].astype(F32) + ref[3, n].astype(F32))
            for k in range(2):
                parts = [total[8 * k : 8 * k + 8, wide * i : wide * i + wide] for i in range(4)]
                R.e5s[2 * n + k, :, at : at + wide] = jnp.concatenate(parts, 0).astype(BF)
        return carry

    lax.fori_loop(0, 8, fold_step, 0)
    plane_push(K.e5, R.e5s, R.e5r)
    R.e5r[i_me] = R.e5s[i_me]

    def rows_of(ref):
        return lambda xx: ref.at[pl.ds(pl.multiple_of(8 * xx, 8), 8)]

    def to_owners(name, src, dst):
        x_push(name, rows_of(src), dst)
        dst[x] = src[pl.ds(pl.multiple_of(8 * x, 8), 8), :]

    got(K.e1, R.e1r.at[0:15])
    total = plane_sum(R.e1r)
    R.dns[0] = total[:, 0:512]
    R.dns[1] = total[:, 512:1024]
    for k in range(2):
        owner = 2 * c + k

        @pl.when(x != owner)
        def _():
            push((K.dn0, K.dn1)[k], R.dns.at[k], R.dnr.at[x], did(b, owner, t, c), slot=K.dnr)

        later((K.dn0, K.dn1)[k], R.dns.at[k], x != owner)

        @pl.when(x == owner)
        def _():
            R.dnr[x] = R.dns[k]

    x_got(K.tbx, R.tbr)
    R.tbo[...] = (R.tbr[0] + R.tbr[1]) + (R.tbr[2] + R.tbr[3])
    plane_push(K.tbp, R.tbo, R.tbp)
    R.tbp[i_me] = R.tbo[...]

    x_got(K.d1, R.d1r)
    dfirst = sum4(R.d1r)
    n1, i1 = normalize(R.tokh[pl.ds(2 * x, 2)].reshape(128, 512).astype(F32))
    dstream = R.dx1[...] + norm_back(dfirst * scale_up, n1, i1)
    R.gts[...] = dstream.astype(BF).reshape(2, 64, 512)
    push(K.gt, R.gts.at[1 - t], R.g_tok.at[t], partner)
    later(K.gt, R.gts.at[0])
    R.g_tok[t] = R.gts[t]

    x_got(K.gp, R.gpr)
    R.gpo[...] = sum4(R.gpr).astype(BF).reshape(2, 80, 384)
    push(K.gpz, R.gpo.at[1 - t], R.g_pat.at[t], partner)
    later(K.gpz, R.gpo.at[0])
    R.g_pat[t] = R.gpo[t]

    got(K.e3, R.e3r.at[0:15])
    R.u3s[...] = plane_sum(R.e3r)
    to_owners(K.u3, R.u3s, R.u3r)

    got(K.e2, R.e2r.at[0:15])
    R.u2s[:, 0:512] = plane_sum(R.e2r)
    got(K.e4, R.e4r.at[0:15])
    R.u2s[:, 512:1024] = plane_sum(R.e4r)
    to_owners(K.u2, R.u2s, R.u2r)
    got(K.e5, R.e5r.at[0:15])
    total = plane_sum(R.e5r)
    for i in range(4):
        R.u1o[:, 256 * i : 256 * i + 256] = total[8 * i : 8 * i + 8, 0:256]
        R.u1o[:, 1024 + 128 * i : 1152 + 128 * i] = total[8 * i : 8 * i + 8, 256:384]
    sib_push(K.u1z, R.u1o, R.u1z)

    x_got(K.u3, R.u3r)
    sib_push(K.u3z, R.u3r, R.u3z)

    @pl.when(x // 2 == c)
    def _():
        x_got(K.dnr, R.dnr)
        R.dno[...] = (R.dnr[0] + R.dnr[1]) + (R.dnr[2] + R.dnr[3])
        push(K.dnz, R.dno.at[pl.ds(pl.multiple_of(16 - 16 * c, 16), 16)], R.dnz, sibling)

    later(K.dnz, R.dnz, x // 2 == c)
    x_got(K.u2, R.u2r)

    R.u2o[...] = (R.u2r[0] + R.u2r[1]) + (R.u2r[2] + R.u2r[3])
    sib_push(K.u2z, R.u2o, R.u2z)

    got(K.cam, R.camr.at[0:7])
    got(K.tbp, R.tbp.at[0:15])
    wanted = iota((8, 128), 1) == 8 * j + iota((8, 128), 0)
    acc = [jnp.zeros((8, 128), F32) for _ in range(8)]
    vec = jnp.zeros((16, 128), F32)
    for o in range(16):
        row = R.camr[o // 2, pl.ds(8 * (o % 2) + b, 1), :]
        weight = jnp.sum(jnp.where(wanted, row, 0.0), 1, keepdims=True)
        dmod = R.tbp[o, 0:8, :]
        for i in range(8):
            acc[i] = acc[i] + weight * dmod[i : i + 1, :]
        vec = vec + R.tbp[o, 8:24, :]
    for i in range(8):
        R.g_mod[:, 128 * i : 128 * i + 128] = acc[i]
    for v in range(4):
        for i in range(4):
            R.g_vec[v : v + 1, 128 * i : 128 * i + 128] = vec[4 * v + i : 4 * v + i + 1, :]

    def mine(v):
        return jnp.where(c == 0, v[0:4], v[4:8])

    def halves(own, other):
        return jnp.where(c == 0, own, other), jnp.where(c == 0, other, own)

    got(K.u3z, R.u3z)
    for k in range(4):
        total = mine(R.u3r[k] + R.u3z[k])
        for n, ref in enumerate((R.g_query, R.g_key, R.g_value)):
            ref[:, 128 * k : 128 * k + 128] = total[:, 128 * n : 128 * n + 128]
    got(K.u1z, R.u1z)
    for n, part in enumerate(halves(mine(R.u1o[...]), mine(R.u1z[...]))):
        for i in range(8):
            R.g_up[:, 256 * i + 128 * n : 256 * i + 128 * n + 128] = part[:, 128 * i : 128 * i + 128]
        R.g_ckey[:, 256 * n : 256 * n + 256] = part[:, 1024:1280]
        R.g_cvalue[:, 256 * n : 256 * n + 256] = part[:, 1280:1536]

    @pl.when(x // 2 == c)
    def _():
        R.g_down[...] = R.dno[pl.ds(pl.multiple_of(16 * c, 16), 16), :]

    @pl.when(x // 2 != c)
    def _():
        got(K.dnz, R.dnz)
        R.g_down[...] = R.dnz[...]

    got(K.u2z, R.u2z)
    for n, part in enumerate(halves(mine(R.u2o[...]), mine(R.u2z[...]))):
        for k, ref in enumerate((R.g_patch, R.g_cout, R.g_cquery, R.g_out)):
            rows = ref.shape[0]
            ref[:, 256 * n : 256 * n + 256] = part[0:rows, 256 * k : 256 * k + 256]

    got(K.out, R.outs.at[0])
    got(K.gt, R.gts.at[0])
    got(K.gpz, R.gpo.at[0])
    for name, like, when in pending:
        if when is None:
            sent(name, like)
        else:
            pl.when(when)(functools.partial(sent, name, like))


def copies(*refs):
    count = len(OUTPUTS) - 1
    sources, vectors, targets, parts = refs[:count], refs[count], refs[count + 1 : 2 * count + 1], refs[2 * count + 1 :]
    for source, target in zip(sources, targets):
        target[...] = source[...]
    at = 64 * lax.axis_index("batch") + 4 * lax.axis_index("blk")
    wanted = iota((4, 512), 1) == at + iota((4, 512), 0)
    for v, part in enumerate(parts):
        part[...] = jnp.sum(jnp.where(wanted, vectors[v : v + 1, :], 0.0), 1)


def hand_over(arrays):
    spec = pl.BlockSpec(memory_space=pltpu.VMEM)
    shapes = [jax.ShapeDtypeStruct(s, d) for s, d in OUTPUTS.values()][:-1]
    shapes += [jax.ShapeDtypeStruct((4,), F32)] * 4
    return pl.pallas_call(
        copies,
        out_shape=shapes,
        in_specs=[spec] * len(OUTPUTS),
        out_specs=[spec] * len(shapes),
        name="results",
    )(*arrays)


def on_device(
    tokens, patches, camera, counts, grad_out, w_mod, w_query, w_key, w_value, w_out, w_patch,
    c_query, c_key, c_value, c_out, gain_two, bias_two, gain_three, bias_three, w_up, w_down,
):
    vmem = pl.BlockSpec(memory_space=pltpu.VMEM)
    outs = pl.pallas_call(
        kernel,
        out_shape=[jax.ShapeDtypeStruct(s, d) for s, d in OUTPUTS.values()],
        in_specs=[pl.BlockSpec(memory_space=space) for space in INPUTS.values()],
        out_specs=[vmem] * len(OUTPUTS),
        scratch_shapes=[pltpu.VMEM(s, d) for s, d in SCRATCH.values()]
        + [pltpu.SemaphoreType.DMA((len(K),)), pltpu.SemaphoreType.DMA((len(K) + 4,))],
        compiler_params=pltpu.CompilerParams(
            collective_id=0, has_side_effects=True, vmem_limit_bytes=58 << 20
        ),
        name="layer",
    )(
        tokens, patches, camera, counts, grad_out, w_mod, w_query, w_key, w_value, w_out,
        w_patch, c_query, c_key, c_value, c_out, gain_two, bias_two, gain_three, bias_three, w_up, w_down,
    )
    *outs, g_gain_two, g_bias_two, g_gain_three, g_bias_three = hand_over(outs)
    return (*outs[:13], g_gain_two, g_bias_two, g_gain_three, g_bias_three, *outs[13:])


def solution(mesh):
    weight = P("blk", None)
    whole = P(("batch", "blk"), None)
    vector = P(("batch", "blk"))
    rows = P("batch", "blk", None)
    return jax.shard_map(
        on_device,
        mesh=mesh,
        in_specs=(
            rows, rows, P("batch", None), P("batch"), rows,
            *(weight,) * 10, *(P("blk"),) * 4, weight, weight,
        ),
        out_specs=(rows, rows, rows, *(whole,) * 10, *(vector,) * 4, whole, whole),
        check_vma=False,
    )
```

```python
import enum
import functools
import types

import jax
import jax.numpy as jnp
from jax import lax
from jax.experimental import pallas as pl
from jax.experimental.pallas import tpu as pltpu
from jax.sharding import PartitionSpec as P

F32 = jnp.float32
BF = jnp.bfloat16
MESH = pl.DeviceIdType.MESH
EPSILON = 1e-05
BIG_NEG = -1e30
GELU_K = 0.7978845608028654
GELU_C = 0.044715


def dot(left, right):
    return jnp.dot(left, right, preferred_element_type=F32)


def dot_nt(left, right):
    return lax.dot_general(left, right, (((1,), (1,)), ((), ())), preferred_element_type=F32)


def dot_tn(left, right):
    return lax.dot_general(left, right, (((0,), (0,)), ((), ())), preferred_element_type=F32)


def normalize(stream):
    centred = stream - jnp.mean(stream, -1, keepdims=True)
    inverse = lax.rsqrt(jnp.mean(centred * centred, -1, keepdims=True) + EPSILON)
    return centred * inverse, inverse


def norm_back(dnormed, normed, inverse):
    return inverse * (
        dnormed
        - jnp.mean(dnormed, -1, keepdims=True)
        - normed * jnp.mean(dnormed * normed, -1, keepdims=True)
    )


def column_sum(rows):
    return jnp.sum(rows, 0, keepdims=True)


def iota(shape, dim):
    return lax.broadcasted_iota(jnp.int32, shape, dim)


class Inputs:
    tok = pltpu.VMEM
    pat = pltpu.VMEM
    camera = pltpu.VMEM
    counts = pltpu.SMEM
    go = pltpu.VMEM
    w_mod = pltpu.VMEM
    w_query = pltpu.VMEM
    w_key = pltpu.VMEM
    w_value = pltpu.VMEM
    w_out = pltpu.VMEM
    w_patch = pltpu.VMEM
    c_query = pltpu.VMEM
    c_key = pltpu.VMEM
    c_value = pltpu.VMEM
    c_out = pltpu.VMEM
    gain_two = pltpu.VMEM
    bias_two = pltpu.VMEM
    gain_three = pltpu.VMEM
    bias_three = pltpu.VMEM
    w_up = pltpu.VMEM
    w_down = pltpu.VMEM


class Outputs:
    out_tok = ((2, 64, 512), BF)
    g_tok = ((2, 64, 512), BF)
    g_pat = ((2, 80, 384), BF)
    g_mod = ((8, 1024), F32)
    g_query = ((4, 512), F32)
    g_key = ((4, 512), F32)
    g_value = ((4, 512), F32)
    g_out = ((4, 512), F32)
    g_patch = ((3, 512), F32)
    g_cquery = ((4, 512), F32)
    g_ckey = ((4, 512), F32)
    g_cvalue = ((4, 512), F32)
    g_cout = ((4, 512), F32)
    g_up = ((4, 2048), F32)
    g_down = ((16, 512), F32)
    g_vec = ((4, 512), F32)


class Scratch:
    cam = ((16, 128), F32)
    tokh = ((8, 64, 512), BF)
    path = ((8, 80, 384), BF)
    wqs = ((4, 32, 384), BF)
    wfs = ((32, 1152), BF)
    wqkv = ((8, 2, 32, 384), BF)
    wf = ((8, 2, 32, 1152), BF)
    mods = ((2, 8, 128), F32)
    modr = ((8, 8, 128), F32)
    modo = ((8, 128), F32)
    modx = ((8, 128), F32)
    camr = ((8, 16, 128), F32)
    gv = ((8, 512), F32)
    bias = ((1280, 128), F32)
    n1h = ((4, 128, 512), F32)
    a1h = ((4, 128, 512), BF)
    qs = ((4, 128, 128), BF)
    kv = ((2, 4, 128, 256), BF)
    p1 = ((4, 1024, 256), BF)
    o1s = ((4, 128, 128), BF)
    o1r = ((4, 128, 128), BF)
    x1 = ((128, 512), F32)
    n2 = ((128, 512), F32)
    i2 = ((128, 128), F32)
    a2 = ((128, 512), BF)
    wk = ((8, 2, 32, 1536), BF)
    kvc = ((2, 4, 160, 1024), BF)
    p2 = ((4, 1280, 256), BF)
    x2 = ((128, 512), F32)
    n3 = ((128, 512), F32)
    i3 = ((128, 128), F32)
    das = ((128, 512), BF)
    dar = ((128, 512), BF)
    ops = ((128, 512), BF)
    opr = ((128, 512), BF)
    outs = ((2, 64, 512), BF)
    dx2 = ((128, 512), F32)
    dkvc = ((2, 4, 160, 1024), BF)
    dkcr = ((4, 160, 1024), BF)
    gps = ((4, 160, 384), BF)
    gpr = ((4, 160, 384), BF)
    gpo = ((2, 80, 384), BF)
    dx1 = ((128, 512), F32)
    do1s = ((4, 128, 128), BF)
    do1r = ((4, 128, 128), BF)
    dkv = ((2, 512, 256), F32)
    dkvs = ((512, 256), BF)
    dkvr = ((512, 256), BF)
    dqkv = ((512, 384), BF)
    d1s = ((4, 128, 512), BF)
    d1r = ((4, 128, 512), BF)
    gts = ((2, 64, 512), BF)
    dq = ((4, 128, 128), BF)
    gb2 = ((512, 512), F32)
    gbs = ((512, 512), BF)
    gbr = ((512, 512), BF)
    gc = ((512, 384), F32)
    e1s = ((16, 32, 1024), BF)
    e1r = ((16, 32, 1024), BF)
    e2s = ((16, 32, 512), BF)
    e2r = ((16, 32, 512), BF)
    e3s = ((16, 32, 384), BF)
    e3r = ((16, 32, 384), BF)
    u1o = ((8, 1536), F32)
    u1z = ((8, 1536), F32)
    dns = ((2, 32, 512), F32)
    dnr = ((4, 32, 512), F32)
    dnz = ((16, 512), F32)
    u2s = ((32, 1024), F32)
    u2r = ((4, 8, 1024), F32)
    u2o = ((8, 1024), F32)
    u2z = ((8, 1024), F32)
    u3s = ((32, 384), F32)
    u3r = ((4, 8, 384), F32)
    u3z = ((4, 8, 384), F32)
    tb = ((24, 128), F32)
    tbs = ((24, 128), F32)
    tbx = ((24, 128), F32)
    tbr = ((4, 24, 128), F32)
    tbo = ((24, 128), F32)
    tbp = ((16, 24, 128), F32)
    wks = ((32, 1536), BF)
    kt = ((128, 1024), BF)
    vt = ((128, 1024), BF)
    wp = ((384, 512), BF)
    pp = ((4, 160, 512), BF)
    qc = ((4, 128, 128), BF)
    o2 = ((4, 128, 128), BF)
    do2 = ((4, 128, 128), BF)
    dqc = ((4, 128, 128), BF)
    dks = ((4, 160, 1024), BF)
    dpp = ((4, 160, 512), BF)
    w3s = ((32, 1024), BF)
    w3m = ((2, 32, 1024), BF)
    w3 = ((8, 2, 32, 1024), BF)
    w4 = ((8, 128, 512), BF)
    go2 = ((2, 2, 64, 512), BF)
    a32 = ((2, 128, 512), BF)
    g2 = ((2, 128, 1024), BF)
    du2 = ((2, 128, 1024), BF)
    dao = ((128, 512), F32)
    oo = ((128, 512), F32)
    dno = ((32, 512), F32)
    gus = ((8, 4, 16, 1024), BF)
    gur = ((4, 8, 16, 1024), BF)
    ga = ((512, 1024), F32)
    gas = ((512, 1024), BF)
    gar = ((512, 1024), BF)
    e4s = ((16, 32, 512), BF)
    e4r = ((16, 32, 512), BF)
    co = ((8, 2, 32, 512), BF)
    kxs = ((8, 4, 16, 512), BF)
    kxr = ((4, 8, 16, 512), BF)
    e5s = ((16, 32, 384), BF)
    e5r = ((16, 32, 384), BF)


def members(group):
    return {name: value for name, value in vars(group).items() if not name.startswith("_")}


INPUTS, OUTPUTS, SCRATCH = members(Inputs), members(Outputs), members(Scratch)


class K(enum.IntEnum):
    a3 = 0
    cam = 1
    d1 = 2
    da = 3
    dkc = 4
    dkv = 5
    dn0 = 6
    dn1 = 7
    dnr = 8
    dnz = 9
    do1 = 10
    e1 = 11
    e2 = 12
    e3 = 13
    e4 = 14
    e5 = 15
    ga = 16
    gb = 17
    gk = 18
    go = 19
    gox = 20
    gp = 21
    gpz = 22
    gt = 23
    kv = 24
    kvc = 25
    kx = 26
    mod = 27
    modx = 28
    o1 = 29
    op = 30
    out = 31
    pat = 32
    tbp = 33
    tbs = 34
    tbx = 35
    tok = 36
    u1z = 37
    u2 = 38
    u2z = 39
    u3 = 40
    u3z = 41
    ux = 42
    w1a = 43
    w1b = 44
    w1c = 45
    w1d = 46
    w2a = 47
    w2b = 48
    w2c = 49
    w2d = 50
    w3 = 51
    w3x = 52
    w4a = 53
    w4b = 54
    w4c = 55
    w5 = 56
    w5d = 57
    wq = 58
    wqx = 59


def kernel(*refs):
    *buffers, ss, rs = refs
    R = types.SimpleNamespace(**dict(zip((*INPUTS, *OUTPUTS, *SCRATCH), buffers)))
    b = lax.axis_index("batch")
    j = lax.axis_index("blk")
    x = j // 4
    t = (j // 2) % 2
    c = j % 2
    p = 2 * x + t
    i_me = 2 * b + t

    def did(bb, xx, tt, cc):
        return (bb, xx * 4 + tt * 2 + cc)

    pending = []
    do1_base = len(K)

    def push(name, src, dst, dev, slot=None):
        pltpu.make_async_remote_copy(
            src_ref=src,
            dst_ref=dst,
            send_sem=ss.at[name],
            recv_sem=rs.at[name if slot is None else slot],
            device_id=dev,
            device_id_type=MESH,
        ).start()

    def got(name, like):
        pltpu.make_async_copy(like, like, rs.at[name]).wait()

    def sent(name, like):
        pltpu.make_async_copy(like, like, ss.at[name]).wait()

    def later(name, like, when=None):
        pending.append((name, like, when))

    sibling = did(b, x, t, 1 - c)
    partner = did(b, x, 1 - t, c)
    near = [((x + dx) % 4, (t + dt) % 2) for dx, dt in ((0, 1), (1, 0), (3, 0), (2, 0), (1, 1), (3, 1), (2, 1))]

    def near_push(name, src_of, dst, like):
        for xx, tt in near:
            push(name, src_of(xx, tt), dst, did(b, xx, tt, c))
        later(name, like)

    def x_push(name, src_of, dst_ref):
        for d in (1, 3, 2):
            xx = (x + d) % 4
            push(name, src_of(xx), dst_ref.at[x], did(b, xx, t, c))
        later(name, dst_ref.at[0:3])

    def x_got(name, dst_ref):
        got(name, dst_ref.at[0:3])

    def sib_push(name, src, dst):
        push(name, src, dst, sibling)
        later(name, dst)

    def plane_push(name, src, dst):
        def step(n, carry):
            bb = (b + n // 2) % 8
            tt = (t + n % 2) % 2
            pltpu.make_async_remote_copy(
                src_ref=src.at[2 * bb + tt] if src.shape[0] == 16 else src,
                dst_ref=dst.at[i_me],
                send_sem=ss.at[name],
                recv_sem=rs.at[name],
                device_id=did(bb, x, tt, c),
                device_id_type=MESH,
            ).start()
            return carry

        lax.fori_loop(1, 16, step, 0)
        later(name, dst.at[0:15])

    def plane_sum(ref):
        def step(n, acc):
            return acc + ref[n].astype(F32)

        return lax.fori_loop(1, 16, step, ref[0].astype(F32))

    for i in range(4):
        cols = slice(128 * i, 128 * i + 128)
        R.wqs[i, :, 0:128] = R.w_query[:, cols]
        R.wqs[i, :, 128:256] = R.w_key[:, cols]
        R.wqs[i, :, 256:384] = R.w_value[:, cols]
    lanes = iota((1, 128), 1)
    half = jnp.where(lanes // 64 == c, 1.0, 0.0).astype(F32)
    for o in range(2):
        for i in range(8):
            R.cam[8 * o + i : 8 * o + i + 1, :] = R.camera[o : o + 1, 128 * i : 128 * i + 128].astype(F32)
    row0 = R.cam[pl.ds(j // 2, 1), :] * half
    row1 = R.cam[pl.ds(8 + j // 2, 1), :] * half
    rows = jnp.concatenate([row0, row1, jnp.zeros((14, 128), F32)], 0).astype(BF)
    w_mod = R.w_mod[...]
    modp = dot(rows, jnp.concatenate([w_mod, w_mod], 0))
    for i in range(8):
        R.mods[0, i : i + 1, :] = modp[0:1, 128 * i : 128 * i + 128]
        R.mods[1, i : i + 1, :] = modp[1:2, 128 * i : 128 * i + 128]

    bar = pltpu.get_barrier_semaphore()

    def greet(dev):
        pl.semaphore_signal(bar, inc=1, device_id=dev, device_id_type=MESH)

    for xx, tt in near:
        greet(did(b, xx, tt, c))
    greet(sibling)

    def greet_plane(n, carry):
        greet(did((b + n // 2) % 8, x, (t + n % 2) % 2, c))
        return carry

    lax.fori_loop(1, 16, greet_plane, 0)

    pl.semaphore_wait(bar, 7 + 1 + 15)

    near_push(K.mod, lambda xx, tt: R.mods.at[tt], R.modr.at[p], R.modr.at[0:7])
    near_push(K.tok, lambda xx, tt: R.tok.at[tt], R.tokh.at[p], R.tokh.at[0:7])
    near_push(K.wq, lambda xx, tt: R.wqs.at[xx], R.wqkv.at[p, c], R.wqkv.at[0:7, 0])

    y = b % 4
    xs = (x + y) % 4
    xd = (x + 4 - y) % 4

    def spread_first(same, cross, src, whole):
        push(cross, src, slot(whole, p), did(b, xd, 1 - t, c))
        later(cross, src)

        @pl.when(y > 0)
        def _():
            push(same, src, slot(whole, p), did(b, xd, t, c))

        later(same, src, y > 0)

        @pl.when(y == 0)
        def _():
            slot(whole, p)[...] = src[...]

    def spread_second(same, cross, name, whole):
        got(cross, slot(whole, 0))

        @pl.when(y > 0)
        def _():
            got(same, slot(whole, 0))

        held = slot(whole, pl.ds(2 * xs, 2))
        for d in (2, 1, 3):
            push(name, held, held, did(b - y + (y + d) % 4, x, t, c))
        later(name, slot(whole, slice(0, 6)))

    def slot(whole, at):
        return whole.at[at, c] if len(whole.shape) == 4 else whole.at[at]

    def spread_third(name, whole):
        got(name, slot(whole, slice(0, 6)))

    def spread_last(name, whole):
        sib_push(name, whole.at[:, c], whole.at[:, c])

    f = iota((32, 24), 1)
    apart = jnp.where(iota((32, 24), 0) == f + (f * 21846) // 65536, 1.0, 0.0).astype(BF)
    R.wks[:, 0:512] = R.c_key[...]
    R.wks[:, 512:1024] = R.c_value[...]
    R.wks[:, 1024:1536] = dot(apart, R.w_patch[...]).astype(BF)
    R.wfs[:, 0:512] = R.w_out[...]
    R.wfs[:, 512:1024] = R.c_query[...]
    row = jnp.zeros((1, 128), F32)
    for v, ref in enumerate((R.gain_two, R.bias_two, R.gain_three, R.bias_three)):
        place = jnp.where(iota((32, 128), 1) == 32 * v + iota((32, 128), 0), 1.0, 0.0).astype(BF)
        row = row + dot(ref[...].reshape(1, 32), place)
    R.wfs[:, 1024:1152] = jnp.broadcast_to(row, (32, 128)).astype(BF)
    for i in range(8):
        left, right = R.w_up[:, 256 * i : 256 * i + 128], R.w_up[:, 256 * i + 128 : 256 * i + 256]
        R.w3s[:, 128 * i : 128 * i + 128] = jnp.where(c == 0, right, left)
        R.w3m[c, :, 128 * i : 128 * i + 128] = jnp.where(c == 0, left, right)
    sib_push(K.w3x, R.w3s, R.w3m.at[c])

    R.modr[p] = R.mods[t]
    R.co[p, c] = R.c_out[...]
    R.tokh[p] = R.tok[t]
    R.wqkv[p, c] = R.wqs[x]
    R.path[p] = R.pat[t]
    R.go2[c, t] = R.go[t]
    R.camr[b] = R.cam[...]

    got(K.mod, R.modr.at[0:7])
    spread_first(K.w1a, K.w1b, R.wks, R.wk)
    spread_first(K.w2a, K.w2b, R.wfs, R.wf)
    spread_first(K.w4a, K.w4b, R.w_down, R.w4)
    R.modo[...] = jnp.sum(R.modr[...], 0)
    sib_push(K.modx, R.modo, R.modx)

    got(K.wq, R.wqkv.at[0:7, 0])
    sib_push(K.wqx, R.wqkv.at[:, c], R.wqkv.at[:, c])

    got(K.tok, R.tokh.at[0:7])

    def norm_step(i, carry):
        R.n1h[i] = normalize(R.tokh[pl.ds(2 * i, 2)].reshape(128, 512).astype(F32))[0]
        return carry

    lax.fori_loop(0, 4, norm_step, 0)

    got(K.modx, R.modx)
    modv = R.modo[...] + R.modx[...]
    scale_up = 1.0 + jnp.concatenate([modv[i : i + 1, :] for i in range(4)], 1)
    shift = jnp.concatenate([modv[i : i + 1, :] for i in range(4, 8)], 1)
    got(K.wqx, R.wqkv.at[:, 0])

    def qkv_step(i, carry):
        a1 = (R.n1h[i] * scale_up + shift).astype(BF)
        R.a1h[i] = a1
        qkv = dot(a1, R.wqkv[...].reshape(512, 384))
        R.qs[i] = (qkv[:, 0:128].astype(BF).astype(F32) * 0.125).astype(BF)
        R.kv[c, i] = qkv[:, 128:384].astype(BF)
        return carry

    spread_second(K.w1a, K.w1b, K.w1c, R.wk)
    lax.fori_loop(0, 4, qkv_step, 0)
    sib_push(K.kv, R.kv.at[c], R.kv.at[c])
    spread_second(K.w2a, K.w2b, K.w2c, R.wf)
    near_push(K.pat, lambda xx, tt: R.pat.at[tt], R.path.at[p], R.path.at[0:7])
    near_push(K.w5, lambda xx, tt: R.c_out, R.co.at[p, c], R.co.at[0:7, 0])
    push(K.go, R.go.at[1 - t], R.go2.at[c, t], partner)
    later(K.go, R.go.at[0])

    def cam_step(n, carry):
        pltpu.make_async_remote_copy(
            src_ref=R.cam,
            dst_ref=R.camr.at[b],
            send_sem=ss.at[K.cam],
            recv_sem=rs.at[K.cam],
            device_id=did((b + n) % 8, x, t, c),
            device_id_type=MESH,
        ).start()
        return carry
    lax.fori_loop(1, 8, cam_step, 0)
    later(K.cam, R.camr.at[0:7])

    eye = jnp.where(iota((128, 128), 0) == iota((128, 128), 1), 1.0, 0.0).astype(BF)
    mask0 = jnp.where(iota((1, 128), 1) < 64, 1.0, 0.0).astype(BF)
    mask1 = jnp.where(iota((1, 128), 1) < 64, 0.0, 1.0).astype(BF)

    def transposed(rows):
        return dot_nt(eye, rows).astype(BF)

    def two_heads(rows):
        return jnp.concatenate([rows * mask0, rows * mask1], 0)

    def unfold(columns):
        return jnp.concatenate([columns[0:64, 0:128], columns[64:128, 128:256]], 0).T

    def attend(queries, keys, values_t, off):
        scores = dot_nt(keys, two_heads(queries))
        if off is not None:
            scores = scores + jnp.concatenate([off, off], 1)
        raised = jnp.exp(scores - jnp.max(scores, 0, keepdims=True))
        weights = (raised * (1.0 / jnp.sum(raised, 0, keepdims=True))).astype(BF)
        return weights, unfold(dot(values_t, weights)).astype(BF)

    def attend_back(queries, douts, keys_t, values, weights_low):
        q, dout = two_heads(queries), two_heads(douts)
        weights = weights_low.astype(F32)
        dweights = dot_nt(values, dout)
        delta = jnp.sum(weights * dweights, 0, keepdims=True)
        dscores = (weights * (dweights - delta)).astype(BF)
        dquery = (unfold(dot(keys_t, dscores)) * 0.125).astype(BF)
        return dquery, dot(dscores, q), dot(weights_low, dout)

    def own_columns(ref):
        return jnp.concatenate([ref[i] for i in range(4)], 1)

    got(K.kv, R.kv.at[0])

    def self_keys():
        return R.kv[:, :, :, 0:128].reshape(1024, 128)

    def self_values():
        return R.kv[:, :, :, 128:256].reshape(1024, 128)

    R.kt[...] = transposed(self_keys())
    R.vt[...] = transposed(self_values())

    def self_step(n, carry):
        xc = (x + 2 + 3 * n + (n // 2) * (7 - 2 * n)) % 4
        weights, out = attend(R.qs[xc], self_keys(), R.vt[...], None)
        R.p1[xc] = weights
        R.o1s[xc] = out

        @pl.when(n < 3)
        def _():
            push(K.o1, R.o1s.at[xc], R.o1r.at[x], did(b, xc, t, c))

        return carry

    lax.fori_loop(0, 4, self_step, 0)
    later(K.o1, R.o1r.at[0:3])
    R.o1r[x] = R.o1s[x]

    spread_third(K.w2c, R.wf)
    spread_last(K.w2d, R.wf)
    spread_second(K.w4a, K.w4b, K.w4c, R.w4)
    got(K.w3x, R.w3s)
    R.w3[p] = R.w3m[...]
    near_push(K.w3, lambda xx, tt: R.w3m, R.w3.at[p], R.w3.at[0:7])
    spread_third(K.w1c, R.wk)
    spread_last(K.w1d, R.wk)
    got(K.go, R.go2.at[0, 0])
    sib_push(K.gox, R.go2.at[c], R.go2.at[c])

    live = R.counts[t]
    for cc in range(2):
        for pp in range(8):
            slots = iota((80, 128), 0) + 80 * (2 * pp + cc)
            R.bias[640 * cc + 80 * pp : 640 * cc + 80 * pp + 80, :] = jnp.where(slots < live, 0.0, BIG_NEG)

    def w_out():
        return R.wf[:, :, :, 0:512].reshape(512, 512)

    def c_query():
        return R.wf[:, :, :, 512:1024].reshape(512, 512)

    def c_out():
        return R.co[...].reshape(512, 512)

    def c_pair():
        return R.wk[:, :, :, 0:1024].reshape(512, 1024)

    def spread_rows():
        f = iota((384, 512), 0)
        return jnp.where(iota((384, 512), 1) == f + (f * 21846) // 65536, 1.0, 0.0).astype(BF)

    got(K.w1d, R.wk.at[:, 0])
    R.wp[...] = dot(spread_rows(), R.wk[:, :, :, 1024:1536].reshape(512, 512)).astype(BF)
    got(K.pat, R.path.at[0:7])

    def patch_step(i, carry):
        projected = dot(R.path[pl.ds(2 * i, 2)].reshape(160, 384), R.wp[...]).astype(BF)
        R.pp[i] = projected
        R.kvc[c, i] = dot(projected, c_pair()).astype(BF)
        push(K.kvc, R.kvc.at[c, i], R.kvc.at[c, i], sibling)
        return carry

    lax.fori_loop(0, 4, patch_step, 0)
    later(K.kvc, R.kvc.at[0])

    got(K.w2d, R.wf.at[:, 0])
    packed = R.wf[:, :, :, 1024:1152].reshape(512, 128)
    pick = jnp.where(iota((16, 512), 1) == 32 * iota((16, 512), 0), 1.0, 0.0).astype(BF)
    vectors = dot(pick, packed).astype(BF)
    for v in range(4):
        spread = jnp.where(iota((128, 512), 0) == 32 * v + iota((128, 512), 1) % 32, 1.0, 0.0).astype(BF)
        placed = jnp.where(iota((16, 512), 1) // 32 == iota((16, 512), 0), dot(vectors, spread), 0.0)
        R.gv[v : v + 1, :] = column_sum(placed)

    x_got(K.o1, R.o1r)
    x1 = R.tokh[pl.ds(2 * x, 2)].reshape(128, 512).astype(F32) + dot(own_columns(R.o1r), w_out())
    R.x1[...] = x1
    n2, i2 = normalize(x1)
    R.n2[...] = n2
    R.i2[...] = jnp.broadcast_to(i2, (128, 128))
    a2 = (n2 * R.gv[0:1, :] + R.gv[1:2, :]).astype(BF)
    R.a2[...] = a2
    qc = (dot(a2, c_query()).astype(BF).astype(F32) * 0.125).astype(BF)
    for i in range(4):
        R.qc[i] = qc[:, 128 * i : 128 * i + 128]


    got(K.kvc, R.kvc.at[0])

    def cross_pair(i):
        keys = R.kvc[:, :, :, pl.ds(pl.multiple_of(128 * i, 128), 128)].reshape(1280, 128)
        values = R.kvc[:, :, :, pl.ds(pl.multiple_of(512 + 128 * i, 128), 128)].reshape(1280, 128)
        return keys, values

    def cross_step(i, carry):
        keys, values = cross_pair(i)
        R.p2[i], R.o2[i] = attend(R.qc[i], keys, transposed(values), R.bias[...])
        return carry

    lax.fori_loop(0, 4, cross_step, 0)
    got(K.w5, R.co.at[0:7, 0])
    spread_last(K.w5d, R.co)
    got(K.w5d, R.co.at[:, 0])
    x2 = R.x1[...] + dot(own_columns(R.o2), c_out())
    R.x2[...] = x2
    n3, i3 = normalize(x2)
    R.n3[...] = n3
    R.i3[...] = jnp.broadcast_to(i3, (128, 128))
    a3 = (n3 * R.gv[2:3, :] + R.gv[3:4, :]).astype(BF)
    R.a32[c] = a3
    sib_push(K.a3, R.a32.at[c], R.a32.at[c])

    got(K.w3, R.w3.at[0:7])
    spread_third(K.w4c, R.w4)
    got(K.gox, R.go2.at[0])

    def w_up():
        return R.w3[...].reshape(512, 1024)

    def w_down():
        return R.w4[...].reshape(1024, 512)

    def perceptron(cc):
        u = dot(R.a32[cc], w_up()).astype(BF).astype(F32)
        dg = dot_nt(R.go2[cc].reshape(128, 512), w_down()).astype(BF).astype(F32)
        th = jnp.tanh(GELU_K * (u + GELU_C * u * u * u))
        R.g2[cc] = (0.5 * u * (1.0 + th)).astype(BF)
        slope = 0.5 * (1.0 + th) + 0.5 * u * (1.0 - th * th) * (GELU_K * (1.0 + 3.0 * GELU_C * u * u))
        du = (dg * slope).astype(BF)
        R.du2[cc] = du
        return dot_nt(du, w_up())

    R.dao[...] = perceptron(c)
    got(K.a3, R.a32.at[0])
    R.das[...] = perceptron(1 - c).astype(BF)
    sib_push(K.da, R.das, R.dar)
    R.ops[...] = dot(R.g2[1 - c], w_down()).astype(BF)
    sib_push(K.op, R.ops, R.opr)
    R.oo[...] = dot(R.g2[c], w_down())

    def pack_rows(read, lo, hi, dst):
        def step(n, carry):
            base = 64 * (n // 2) + 8 * (n % 2)
            parts = [read[pl.ds(pl.multiple_of(base + 16 * k, 8), 8), lo:hi] for k in range(4)]
            dst[n] = jnp.concatenate(parts, 0).astype(BF)
            return carry

        lax.fori_loop(0, 16, step, 0)

    R.gus[...] = dot_tn(R.a32[...].reshape(256, 512), R.du2[...].reshape(256, 1024)).astype(BF).reshape(8, 4, 16, 1024)
    x_push(K.ux, lambda xx: R.gus.at[:, xx], R.gur)
    R.gur[x] = R.gus[:, x]
    for i in range(8):
        grad = dot_tn(R.g2[:, :, 128 * i : 128 * i + 128].reshape(256, 128), R.go2[...].reshape(256, 512)).astype(BF)
        for k in range(4):
            R.e1s[2 * i + k % 2, :, 512 * (k // 2) : 512 * (k // 2) + 512] = grad[32 * k : 32 * k + 32]

    plane_push(K.e1, R.e1s, R.e1r)
    R.e1r[i_me] = R.e1s[i_me]

    def sum4(ref):
        return (ref[0].astype(F32) + ref[1].astype(F32)) + (ref[2].astype(F32) + ref[3].astype(F32))

    def put_vector(at, row):
        for i in range(4):
            R.tb[at + i : at + i + 1, :] = row[:, 128 * i : 128 * i + 128]

    def put_halves(own, other, at, grad):
        width = grad.shape[1] // 2
        left, right = grad[:, 0:width], grad[:, width : 2 * width]
        own[:, at : at + width] = jnp.where(c == 0, left, right)
        other[:, at : at + width] = jnp.where(c == 0, right, left).astype(BF)

    got(K.da, R.dar)
    dthird = R.dao[...] + R.dar[...].astype(F32)
    n3 = R.n3[...]
    put_vector(16, column_sum(dthird * n3))
    put_vector(20, column_sum(dthird))
    dy = R.go2[c].reshape(128, 512).astype(F32)
    dx2 = dy + norm_back(dthird * R.gv[2:3, :], n3, R.i3[:, 0:1])
    R.dx2[...] = dx2
    dx2_low = dx2.astype(BF)
    do2 = dot_nt(dx2_low, c_out()).astype(BF)
    for i in range(4):
        R.do2[i] = do2[:, 128 * i : 128 * i + 128]

    def cross_back(i, carry):
        keys, values = cross_pair(i)
        R.dqc[i], dk, dv = attend_back(R.qc[i], R.do2[i], transposed(keys), values, R.p2[i])
        R.dkvc[:, :, :, pl.ds(pl.multiple_of(128 * i, 128), 128)] = dk.astype(BF).reshape(2, 4, 160, 128)
        R.dkvc[:, :, :, pl.ds(pl.multiple_of(512 + 128 * i, 128), 128)] = dv.astype(BF).reshape(2, 4, 160, 128)
        for k in range(2):
            part = pl.ds(pl.multiple_of(512 * k + 128 * i, 128), 128)
            push(K.dkc, R.dkvc.at[1 - c, :, :, part], R.dkcr.at[:, :, part], sibling)
        return carry

    lax.fori_loop(0, 4, cross_back, 0)
    later(K.dkc, R.dkcr)

    dqc = own_columns(R.dqc)
    dsecond = dot_nt(dqc, c_query())
    n2 = R.n2[...]
    put_vector(8, column_sum(dsecond * n2))
    put_vector(12, column_sum(dsecond))
    dx1 = R.dx2[...] + norm_back(dsecond * R.gv[0:1, :], n2, R.i2[:, 0:1])
    R.dx1[...] = dx1
    dx1_low = dx1.astype(BF)
    do1 = dot_nt(dx1_low, w_out()).astype(BF)
    for i in range(4):
        R.do1s[i] = do1[:, 128 * i : 128 * i + 128]
    for d in (2, 1, 3):
        xx = (x + d) % 4
        push(K.do1, R.do1s.at[xx], R.do1r.at[x], did(b, xx, t, c), slot=do1_base + x)
    later(K.do1, R.do1r.at[0:3])
    R.do1r[x] = R.do1s[x]

    got(K.op, R.opr)
    R.outs[...] = (R.x2[...] + R.oo[...] + R.opr[...].astype(F32)).astype(BF).reshape(2, 64, 512)
    push(K.out, R.outs.at[1 - t], R.out_tok.at[t], partner)
    later(K.out, R.outs.at[0])
    R.out_tok[t] = R.outs[t]

    got(K.dkc, R.dkcr)

    def patch_back(i, carry):
        dkv = (R.dkvc[c, i].astype(F32) + R.dkcr[i].astype(F32)).astype(BF)
        R.dks[i] = dkv
        dpp = dot_nt(dkv, c_pair()).astype(BF)
        R.dpp[i] = dpp
        R.gps[i] = dot_nt(dpp, R.wp[...]).astype(BF)

        @pl.when(i != x)
        def _():
            push(K.gp, R.gps.at[i], R.gpr.at[x], did(b, i, t, c))

        return carry

    lax.fori_loop(0, 4, patch_back, 0)
    later(K.gp, R.gpr.at[0:3])
    R.gpr[x] = R.gps[x]
    grad = dot_tn(R.pp[...].reshape(640, 512), R.dks[...].reshape(640, 1024))
    put_halves(R.ga, R.gas, 0, grad[:, 0:512])
    put_halves(R.ga, R.gas, 256, grad[:, 512:1024])
    sib_push(K.gk, R.gas.at[:, 0:512], R.gar.at[:, 0:512])
    spread = dot(R.path[...].reshape(640, 384), spread_rows()).astype(BF)
    put_halves(R.ga, R.gas, 512, dot_tn(spread, R.dpp[...].reshape(640, 512)))
    put_halves(R.ga, R.gas, 768, dot_tn(own_columns(R.o2), R.dx2[...].astype(BF)))
    sib_push(K.ga, R.gas.at[:, 512:1024], R.gar.at[:, 512:1024])
    put_halves(R.gb2, R.gbs, 0, dot_tn(R.a2[...], dqc))
    put_halves(R.gb2, R.gbs, 256, dot_tn(own_columns(R.o1r), dx1_low))
    sib_push(K.gb, R.gbs, R.gbr)
    got(K.gk, R.gar.at[:, 0:512])
    R.kxs[...] = (R.ga[:, 0:512] + R.gar[:, 0:512].astype(F32)).astype(BF).reshape(8, 4, 16, 512)
    x_push(K.kx, lambda xx: R.kxs.at[:, xx], R.kxr)
    R.kxr[x] = R.kxs[:, x]
    got(K.ga, R.gar.at[:, 512:1024])
    R.ga[:, 512:1024] += R.gar[:, 512:1024].astype(F32)
    pack_rows(R.ga, 512, 1024, R.e2s)
    plane_push(K.e2, R.e2s, R.e2r)
    R.e2r[i_me] = R.e2s[i_me]
    got(K.gb, R.gbr)
    R.gb2[...] += R.gbr[...].astype(F32)
    pack_rows(R.gb2, 0, 512, R.e4s)
    plane_push(K.e4, R.e4s, R.e4r)
    R.e4r[i_me] = R.e4s[i_me]

    R.dkv[...] = jnp.zeros(R.dkv.shape, F32)

    def self_back(n, carry):
        xc = (x + 3 * n + (n // 2) * (7 - 2 * n)) % 4

        @pl.when(n > 0)
        def _():
            pltpu.make_async_copy(R.do1r.at[0], R.do1r.at[0], rs.at[do1_base + xc]).wait()

        R.dq[xc], dk, dv = attend_back(R.qs[xc], R.do1r[xc], R.kt[...], self_values(), R.p1[xc])
        R.dkv[:, :, 0:128] += dk.reshape(2, 512, 128)
        R.dkv[:, :, 128:256] += dv.reshape(2, 512, 128)
        return carry

    lax.fori_loop(0, 4, self_back, 0)
    R.dkvs[...] = R.dkv[1 - c].astype(BF)
    sib_push(K.dkv, R.dkvs, R.dkvr)
    R.dqkv[:, 0:128] = R.dq[...].reshape(512, 128)
    R.gc[:, 0:128] = dot_tn(R.a1h[...].reshape(512, 512), R.dqkv[:, 0:128])
    got(K.dkv, R.dkvr)
    R.dqkv[:, 128:384] = (R.dkv[c] + R.dkvr[...].astype(F32)).astype(BF)

    R.gc[:, 128:384] = dot_tn(R.a1h[...].reshape(512, 512), R.dqkv[:, 128:384])
    pack_rows(R.gc, 0, 384, R.e3s)
    plane_push(K.e3, R.e3s, R.e3r)
    R.e3r[i_me] = R.e3s[i_me]

    def first_step(i, sums):
        d1 = dot_nt(R.dqkv[pl.ds(pl.multiple_of(128 * i, 128), 128), :], R.wqkv[...].reshape(512, 384))
        R.d1s[i] = d1.astype(BF)

        @pl.when(i != x)
        def _():
            push(K.d1, R.d1s.at[i], R.d1r.at[x], did(b, i, t, c))

        return sums[0] + column_sum(d1 * R.n1h[i]), sums[1] + column_sum(d1)

    zero = jnp.zeros((1, 512), F32)
    dscale, dshift = lax.fori_loop(0, 4, first_step, (zero, zero))
    later(K.d1, R.d1r.at[0:3])
    R.d1r[x] = R.d1s[x]
    put_vector(0, dscale)
    put_vector(4, dshift)
    sib_push(K.tbs, R.tb, R.tbs)
    got(K.tbs, R.tbs)
    R.tbx[...] = R.tb[...] + R.tbs[...]
    x_push(K.tbx, lambda xx: R.tbx, R.tbr)
    R.tbr[x] = R.tbx[...]

    x_got(K.ux, R.gur)
    x_got(K.kx, R.kxr)

    def fold_step(n, carry):
        for ref, at, wide in ((R.gur, 0, 256), (R.kxr, 256, 128)):
            total = (ref[0, n].astype(F32) + ref[1, n].astype(F32)) + (ref[2, n].astype(F32) + ref[3, n].astype(F32))
            for k in range(2):
                parts = [total[8 * k : 8 * k + 8, wide * i : wide * i + wide] for i in range(4)]
                R.e5s[2 * n + k, :, at : at + wide] = jnp.concatenate(parts, 0).astype(BF)
        return carry

    lax.fori_loop(0, 8, fold_step, 0)
    plane_push(K.e5, R.e5s, R.e5r)
    R.e5r[i_me] = R.e5s[i_me]

    def rows_of(ref):
        return lambda xx: ref.at[pl.ds(pl.multiple_of(8 * xx, 8), 8)]

    def to_owners(name, src, dst):
        x_push(name, rows_of(src), dst)
        dst[x] = src[pl.ds(pl.multiple_of(8 * x, 8), 8), :]

    got(K.e1, R.e1r.at[0:15])
    total = plane_sum(R.e1r)
    R.dns[0] = total[:, 0:512]
    R.dns[1] = total[:, 512:1024]
    for k in range(2):
        owner = 2 * c + k

        @pl.when(x != owner)
        def _():
            push((K.dn0, K.dn1)[k], R.dns.at[k], R.dnr.at[x], did(b, owner, t, c), slot=K.dnr)

        later((K.dn0, K.dn1)[k], R.dns.at[k], x != owner)

        @pl.when(x == owner)
        def _():
            R.dnr[x] = R.dns[k]

    x_got(K.tbx, R.tbr)
    R.tbo[...] = (R.tbr[0] + R.tbr[1]) + (R.tbr[2] + R.tbr[3])
    plane_push(K.tbp, R.tbo, R.tbp)
    R.tbp[i_me] = R.tbo[...]

    x_got(K.d1, R.d1r)
    dfirst = sum4(R.d1r)
    n1, i1 = normalize(R.tokh[pl.ds(2 * x, 2)].reshape(128, 512).astype(F32))
    dstream = R.dx1[...] + norm_back(dfirst * scale_up, n1, i1)
    R.gts[...] = dstream.astype(BF).reshape(2, 64, 512)
    push(K.gt, R.gts.at[1 - t], R.g_tok.at[t], partner)
    later(K.gt, R.gts.at[0])
    R.g_tok[t] = R.gts[t]

    x_got(K.gp, R.gpr)
    R.gpo[...] = sum4(R.gpr).astype(BF).reshape(2, 80, 384)
    push(K.gpz, R.gpo.at[1 - t], R.g_pat.at[t], partner)
    later(K.gpz, R.gpo.at[0])
    R.g_pat[t] = R.gpo[t]

    got(K.e3, R.e3r.at[0:15])
    R.u3s[...] = plane_sum(R.e3r)
    to_owners(K.u3, R.u3s, R.u3r)

    got(K.e2, R.e2r.at[0:15])
    R.u2s[:, 0:512] = plane_sum(R.e2r)
    got(K.e4, R.e4r.at[0:15])
    R.u2s[:, 512:1024] = plane_sum(R.e4r)
    to_owners(K.u2, R.u2s, R.u2r)
    got(K.e5, R.e5r.at[0:15])
    total = plane_sum(R.e5r)
    for i in range(4):
        R.u1o[:, 256 * i : 256 * i + 256] = total[8 * i : 8 * i + 8, 0:256]
        R.u1o[:, 1024 + 128 * i : 1152 + 128 * i] = total[8 * i : 8 * i + 8, 256:384]
    sib_push(K.u1z, R.u1o, R.u1z)

    x_got(K.u3, R.u3r)
    sib_push(K.u3z, R.u3r, R.u3z)

    @pl.when(x // 2 == c)
    def _():
        x_got(K.dnr, R.dnr)
        R.dno[...] = (R.dnr[0] + R.dnr[1]) + (R.dnr[2] + R.dnr[3])
        push(K.dnz, R.dno.at[pl.ds(pl.multiple_of(16 - 16 * c, 16), 16)], R.dnz, sibling)

    later(K.dnz, R.dnz, x // 2 == c)
    x_got(K.u2, R.u2r)

    R.u2o[...] = (R.u2r[0] + R.u2r[1]) + (R.u2r[2] + R.u2r[3])
    sib_push(K.u2z, R.u2o, R.u2z)

    got(K.cam, R.camr.at[0:7])
    got(K.tbp, R.tbp.at[0:15])
    wanted = iota((8, 128), 1) == 8 * j + iota((8, 128), 0)
    acc = [jnp.zeros((8, 128), F32) for _ in range(8)]
    vec = jnp.zeros((16, 128), F32)
    for o in range(16):
        row = R.camr[o // 2, pl.ds(8 * (o % 2) + b, 1), :]
        weight = jnp.sum(jnp.where(wanted, row, 0.0), 1, keepdims=True)
        dmod = R.tbp[o, 0:8, :]
        for i in range(8):
            acc[i] = acc[i] + weight * dmod[i : i + 1, :]
        vec = vec + R.tbp[o, 8:24, :]
    for i in range(8):
        R.g_mod[:, 128 * i : 128 * i + 128] = acc[i]
    for v in range(4):
        for i in range(4):
            R.g_vec[v : v + 1, 128 * i : 128 * i + 128] = vec[4 * v + i : 4 * v + i + 1, :]

    def mine(v):
        return jnp.where(c == 0, v[0:4], v[4:8])

    def halves(own, other):
        return jnp.where(c == 0, own, other), jnp.where(c == 0, other, own)

    got(K.u3z, R.u3z)
    for k in range(4):
        total = mine(R.u3r[k] + R.u3z[k])
        for n, ref in enumerate((R.g_query, R.g_key, R.g_value)):
            ref[:, 128 * k : 128 * k + 128] = total[:, 128 * n : 128 * n + 128]
    got(K.u1z, R.u1z)
    for n, part in enumerate(halves(mine(R.u1o[...]), mine(R.u1z[...]))):
        for i in range(8):
            R.g_up[:, 256 * i + 128 * n : 256 * i + 128 * n + 128] = part[:, 128 * i : 128 * i + 128]
        R.g_ckey[:, 256 * n : 256 * n + 256] = part[:, 1024:1280]
        R.g_cvalue[:, 256 * n : 256 * n + 256] = part[:, 1280:1536]

    @pl.when(x // 2 == c)
    def _():
        R.g_down[...] = R.dno[pl.ds(pl.multiple_of(16 * c, 16), 16), :]

    @pl.when(x // 2 != c)
    def _():
        got(K.dnz, R.dnz)
        R.g_down[...] = R.dnz[...]

    got(K.u2z, R.u2z)
    for n, part in enumerate(halves(mine(R.u2o[...]), mine(R.u2z[...]))):
        for k, ref in enumerate((R.g_patch, R.g_cout, R.g_cquery, R.g_out)):
            rows = ref.shape[0]
            ref[:, 256 * n : 256 * n + 256] = part[0:rows, 256 * k : 256 * k + 256]

    got(K.out, R.outs.at[0])
    got(K.gt, R.gts.at[0])
    got(K.gpz, R.gpo.at[0])
    for name, like, when in pending:
        if when is None:
            sent(name, like)
        else:
            pl.when(when)(functools.partial(sent, name, like))


def copies(*refs):
    count = len(OUTPUTS) - 1
    sources, vectors, targets, parts = refs[:count], refs[count], refs[count + 1 : 2 * count + 1], refs[2 * count + 1 :]
    for source, target in zip(sources, targets):
        target[...] = source[...]
    at = 64 * lax.axis_index("batch") + 4 * lax.axis_index("blk")
    wanted = iota((4, 512), 1) == at + iota((4, 512), 0)
    for v, part in enumerate(parts):
        part[...] = jnp.sum(jnp.where(wanted, vectors[v : v + 1, :], 0.0), 1)


def hand_over(arrays):
    spec = pl.BlockSpec(memory_space=pltpu.VMEM)
    shapes = [jax.ShapeDtypeStruct(s, d) for s, d in OUTPUTS.values()][:-1]
    shapes += [jax.ShapeDtypeStruct((4,), F32)] * 4
    return pl.pallas_call(
        copies,
        out_shape=shapes,
        in_specs=[spec] * len(OUTPUTS),
        out_specs=[spec] * len(shapes),
        name="results",
    )(*arrays)


def on_device(
    tokens, patches, camera, counts, grad_out, w_mod, w_query, w_key, w_value, w_out, w_patch,
    c_query, c_key, c_value, c_out, gain_two, bias_two, gain_three, bias_three, w_up, w_down,
):
    vmem = pl.BlockSpec(memory_space=pltpu.VMEM)
    outs = pl.pallas_call(
        kernel,
        out_shape=[jax.ShapeDtypeStruct(s, d) for s, d in OUTPUTS.values()],
        in_specs=[pl.BlockSpec(memory_space=space) for space in INPUTS.values()],
        out_specs=[vmem] * len(OUTPUTS),
        scratch_shapes=[pltpu.VMEM(s, d) for s, d in SCRATCH.values()]
        + [pltpu.SemaphoreType.DMA((len(K),)), pltpu.SemaphoreType.DMA((len(K) + 4,))],
        compiler_params=pltpu.CompilerParams(
            collective_id=0, has_side_effects=True, vmem_limit_bytes=58 << 20
        ),
        name="layer",
    )(
        tokens, patches, camera, counts, grad_out, w_mod, w_query, w_key, w_value, w_out,
        w_patch, c_query, c_key, c_value, c_out, gain_two, bias_two, gain_three, bias_three, w_up, w_down,
    )
    *outs, g_gain_two, g_bias_two, g_gain_three, g_bias_three = hand_over(outs)
    return (*outs[:13], g_gain_two, g_bias_two, g_gain_three, g_bias_three, *outs[13:])


def solution(mesh):
    weight = P("blk", None)
    whole = P(("batch", "blk"), None)
    vector = P(("batch", "blk"))
    rows = P("batch", "blk", None)
    return jax.shard_map(
        on_device,
        mesh=mesh,
        in_specs=(
            rows, rows, P("batch", None), P("batch"), rows,
            *(weight,) * 10, *(P("blk"),) * 4, weight, weight,
        ),
        out_specs=(rows, rows, rows, *(whole,) * 10, *(vector,) * 4, whole, whole),
        check_vma=False,
    )
```
